32 devices in a mesh: dp: 4 (over y, core), mp: 8 (over z, x).
Axes of the slice: x: 2, y: 2, z: 4, core: 2. Of those that a mesh axis runs over, the one named last changes fastest.
Arguments:
- layer_in: float32 [8192, 2048], P('dp', 'mp'), may hold values from -18 to 18
- out_grad: float32 [8192, 2048], P('dp', 'mp'), may hold values from -6 to 6
- doc_ids: int32 [4, 2048], P('dp'), may hold values from 0 to 7, as said below
- group_owner: int32 [272], replicated, may hold values from 0 to 7, as said below
- norm_gains: float32 [2, 2048], P(None, 'mp'), may hold values from 0.5 to 1.5
- norm_gains_moment: float32 [2, 2048], P(None, 'mp'), may hold values from -768 to 768
- norm_gains_average: float32 [2, 2048], P(None, 'mp'), may hold values from 0.5 to 1.5
- feature_proj: float32 [2048, 2, 256], P('dp', None, 'mp'), may hold values from -0.125 to 0.125
- feature_proj_moment: float32 [2048, 2, 256], P('dp', None, 'mp'), may hold values from -512 to 512
- feature_proj_average: float32 [2048, 2, 256], P('dp', None, 'mp'), may hold values from -0.125 to 0.125
- head_proj: float32 [2048, 4, 2048], P('dp', None, 'mp'), may hold values from -0.125 to 0.125
- head_proj_moment: float32 [2048, 4, 2048], P('dp', None, 'mp'), may hold values from -512 to 512
- head_proj_average: float32 [2048, 4, 2048], P('dp', None, 'mp'), may hold values from -0.125 to 0.125
- mixer_out: float32 [2, 2048, 2048], P(None, 'mp', 'dp'), may hold values from -0.75 to 0.75
- mixer_out_moment: float32 [2, 2048, 2048], P(None, 'mp', 'dp'), may hold values from -112 to 112
- mixer_out_average: float32 [2, 2048, 2048], P(None, 'mp', 'dp'), may hold values from -0.75 to 0.75
- gate_up: float32 [2048, 2, 5632], P('dp', None, 'mp'), may hold values from -0.125 to 0.125
- gate_up_moment: float32 [2048, 2, 5632], P('dp', None, 'mp'), may hold values from -192 to 192
- gate_up_average: float32 [2048, 2, 5632], P('dp', None, 'mp'), may hold values from -0.125 to 0.125
- down_proj: float32 [5632, 2048], P('mp', 'dp'), may hold values from -0.078125 to 0.078125
- down_proj_moment: float32 [5632, 2048], P('mp', 'dp'), may hold values from -320 to 320
- down_proj_average: float32 [5632, 2048], P('mp', 'dp'), may hold values from -0.078125 to 0.078125
Outputs:
- out_y: float32 [8192, 2048], P('dp', 'mp')
- grad_x: float32 [8192, 2048], P('dp', 'mp')
- row_state: float32 [4, 544, 17, 128], P('dp', 'mp')
- norm_gains_grad: float32 [2, 2048], P(None, 'mp')
- norm_gains_new: float32 [2, 2048], P(None, 'mp')
- norm_gains_moment_new: float32 [2, 2048], P(None, 'mp')
- norm_gains_average_new: float32 [2, 2048], P(None, 'mp')
- norm_gains_copy: bfloat16 [2, 2048], P(None, 'mp')
- feature_proj_grad: float32 [2048, 2, 256], P('dp', None, 'mp')
- feature_proj_new: float32 [2048, 2, 256], P('dp', None, 'mp')
- feature_proj_moment_new: float32 [2048, 2, 256], P('dp', None, 'mp')
- feature_proj_average_new: float32 [2048, 2, 256], P('dp', None, 'mp')
- feature_proj_copy: bfloat16 [2048, 2, 256], P('dp', None, 'mp')
- head_proj_grad: float32 [2048, 4, 2048], P('dp', None, 'mp')
- head_proj_new: float32 [2048, 4, 2048], P('dp', None, 'mp')
- head_proj_moment_new: float32 [2048, 4, 2048], P('dp', None, 'mp')
- head_proj_average_new: float32 [2048, 4, 2048], P('dp', None, 'mp')
- head_proj_copy: bfloat16 [2048, 4, 2048], P('dp', None, 'mp')
- mixer_out_grad: float32 [2, 2048, 2048], P(None, 'mp', 'dp')
- mixer_out_new: float32 [2, 2048, 2048], P(None, 'mp', 'dp')
- mixer_out_moment_new: float32 [2, 2048, 2048], P(None, 'mp', 'dp')
- mixer_out_average_new: float32 [2, 2048, 2048], P(None, 'mp', 'dp')
- mixer_out_copy: bfloat16 [2, 2048, 2048], P(None, 'mp', 'dp')
- gate_up_grad: float32 [2048, 2, 5632], P('dp', None, 'mp')
- gate_up_new: float32 [2048, 2, 5632], P('dp', None, 'mp')
- gate_up_moment_new: float32 [2048, 2, 5632], P('dp', None, 'mp')
- gate_up_average_new: float32 [2048, 2, 5632], P('dp', None, 'mp')
- gate_up_copy: bfloat16 [2048, 2, 5632], P('dp', None, 'mp')
- down_proj_grad: float32 [5632, 2048], P('mp', 'dp')
- down_proj_new: float32 [5632, 2048], P('mp', 'dp')
- down_proj_moment_new: float32 [5632, 2048], P('mp', 'dp')
- down_proj_average_new: float32 [5632, 2048], P('mp', 'dp')
- down_proj_copy: bfloat16 [5632, 2048], P('mp', 'dp')
The draws below stay inside these ranges and needn't reach their ends.
Inputs may be any that keep to these rules, and one draw needn't show every extreme that they name: `doc_ids`: within each row the document number starts at 0, rises by one at each new document and never falls; a row holds at most 8 documents, and some row holds exactly 8; each document has 1 to 512 tokens, and at least one document of each row has exactly that many. `group_owner`: exactly one index of mp owns 68 groups; every other index owns (204) // (number of mp indices - 1) groups or one more.
All inputs are finite; a program needn't handle non-finite values.
Results may differ from the reference program's by a relative error of at most 0.025.
Values may be sent and summed in bfloat16 or wider, within the bound.
No kernel may reach another device: no remote copies, remote signals or barrier semaphores. Data moves between devices by JAX's collectives and lax.ppermute only.
A program may use at most 448 MiB of HBM per device.

```python
import math
import jax
import jax.numpy as jnp
from jax import lax

D = 2048
HEADS = 16
FEAT = 16
HV = 128
FF = 5632
WIN = 64
LEN = 2048
F1 = 17
GROUPS = 272
CAP = 68
ROWS = 4
TOKENS = 8192
N_MP = 8


def draw_group_owner(key, part):
    group_key, device_key = jax.random.split(jax.random.fold_in(key, 17))
    order = jax.random.permutation(group_key, GROUPS)
    devices = jax.random.permutation(device_key, N_MP)
    ordinal = jnp.arange(GROUPS, dtype=jnp.int32)
    others = jnp.maximum(ordinal - CAP, 0) % (N_MP - 1) + 1
    device_slot = jnp.where(ordinal < CAP, 0, others)
    owners = devices[device_slot].astype(jnp.int32)
    return jnp.zeros((GROUPS,), jnp.int32).at[order].set(owners)


def document_layout(key):
    layout_key = jax.random.fold_in(key, 31)
    offset_key, flag_key, point_key, forced_key = jax.random.split(layout_key, 4)
    quarter = LEN // 4
    margin = LEN // 32
    offsets = jax.random.randint(offset_key, (ROWS, 1), 1, quarter, dtype=jnp.int32)
    flags = jax.random.randint(flag_key, (ROWS, 4), 0, 2, dtype=jnp.int32)
    first_row = (jnp.arange(ROWS, dtype=jnp.int32)[:, None] == 0).astype(jnp.int32)
    flags = jnp.maximum(flags, first_row)
    points = jax.random.randint(point_key, (ROWS, 4), margin, quarter - margin + 1, dtype=jnp.int32)
    forced = jax.random.randint(forced_key, (ROWS, 1), 0, 3, dtype=jnp.int32)
    quarters = jnp.arange(4, dtype=jnp.int32)[None, :]
    flags = flags * (quarters != forced).astype(jnp.int32)
    starts = offsets + quarter * quarters
    splits = jnp.where(flags > 0, starts + points, 0)
    bounds = jnp.concatenate([starts, splits], axis=1)
    position = jnp.arange(LEN, dtype=jnp.int32)[None, :, None]
    active = (bounds[:, None, :] > 0) & (bounds[:, None, :] <= position)
    ids = jnp.sum(active.astype(jnp.int32), axis=2).astype(jnp.int32)
    begin = jnp.max(jnp.where(active, bounds[:, None, :], 0), axis=2)
    inside = position[:, :, 0] - begin
    return (ids, inside)


def draw_doc_ids(key, part):
    ids, inside = document_layout(key)
    return ids


def draw_layer_in(key, part):
    ids, inside = document_layout(key)
    noise_key, vector_key = jax.random.split(jax.random.fold_in(key, 47))
    noise = jax.random.truncated_normal(noise_key, -6.0, 6.0, (ROWS, LEN, D), jnp.float32)
    strength = 2.0
    vectors = jax.random.truncated_normal(vector_key, -6.0, 6.0, (ROWS, 9, D), jnp.float32)
    picked = vectors[jnp.arange(ROWS)[:, None], ids]
    header = (inside < LEN // 32).astype(jnp.float32)[:, :, None]
    return (noise + strength * header * picked).reshape(ROWS * LEN, D)


def steps_of(own_key, shape, cuts, low, top_value):
    factor_of, own = 1.0, jax.random.fold_in(own_key, 6)
    for dim, shards_of in cuts:
        steps = jnp.exp(jax.random.uniform(jax.random.fold_in(own, dim), (shards_of,), jnp.float32, low / len(cuts), top_value / len(cuts)))
        factor_of = factor_of * jnp.repeat(steps, shape[dim] // shards_of).reshape([-1 if axis == dim else 1 for axis in range(len(shape))])
    return factor_of


def centred(stream_key, dims, deviation, bound, cuts=(), held_as=jnp.bfloat16):
    entries = deviation * jax.random.normal(stream_key, dims, jnp.float32)
    if cuts:
        entries = entries * steps_of(stream_key, dims, cuts, -0.22, 0.18)
    return jnp.clip(entries, -bound, bound).astype(held_as)


def setup_inputs(seed: int = 0) -> dict:
    streams_of = jax.random.split(jax.random.key(seed), 23)
    layer_in = draw_layer_in(jax.random.fold_in(streams_of[22], 71), 0)
    out_grad = centred(streams_of[1], (TOKENS, D), 1.0, 6.0, ((0, 4), (1, 8)), jnp.float32)
    doc_ids = draw_doc_ids(jax.random.fold_in(streams_of[22], 71), 0)
    group_owner = draw_group_owner(jax.random.fold_in(streams_of[22], 71), 0)
    norm_gains = jnp.clip(1.0 + 0.1 * jax.random.normal(streams_of[4], (2, D), jnp.float32), 0.5, 1.5)
    norm_gains_moment = centred(streams_of[5], (2, D), (1.5 * TOKENS ** 0.5), 768.0, ((1, 8),), jnp.float32)
    norm_gains_average = jnp.clip(1.0 + 0.1 * jax.random.normal(streams_of[6], (2, D), jnp.float32), 0.5, 1.5)
    feature_proj = centred(streams_of[7], (D, 2, HEADS * FEAT), D ** -0.5, 0.125, ((0, 4), (2, 8)), jnp.float32)
    feature_proj_moment = centred(streams_of[8], (D, 2, HEADS * FEAT), (1.0 * TOKENS ** 0.5), 512.0, ((0, 4), (2, 8)), jnp.float32)
    feature_proj_average = centred(streams_of[9], (D, 2, HEADS * FEAT), D ** -0.5, 0.125, ((0, 4), (2, 8)), jnp.float32)
    head_proj = centred(streams_of[10], (D, 4, HEADS * HV), D ** -0.5, 0.125, ((0, 4), (2, 8)), jnp.float32)
    head_proj_moment = centred(streams_of[11], (D, 4, HEADS * HV), (1.0 * TOKENS ** 0.5), 512.0, ((0, 4), (2, 8)), jnp.float32)
    head_proj_average = centred(streams_of[12], (D, 4, HEADS * HV), D ** -0.5, 0.125, ((0, 4), (2, 8)), jnp.float32)
    mixer_out = centred(streams_of[13], (2, HEADS * HV, D), 64 ** -0.5, 0.75, ((1, 8), (2, 4)), jnp.float32)
    mixer_out_moment = centred(streams_of[14], (2, HEADS * HV, D), (0.2 * TOKENS ** 0.5), 112.0, ((1, 8), (2, 4)), jnp.float32)
    mixer_out_average = centred(streams_of[15], (2, HEADS * HV, D), 64 ** -0.5, 0.75, ((1, 8), (2, 4)), jnp.float32)
    gate_up = centred(streams_of[16], (D, 2, FF), D ** -0.5, 0.125, ((0, 4), (2, 8)), jnp.float32)
    gate_up_moment = centred(streams_of[17], (D, 2, FF), (0.35 * TOKENS ** 0.5), 192.0, ((0, 4), (2, 8)), jnp.float32)
    gate_up_average = centred(streams_of[18], (D, 2, FF), D ** -0.5, 0.125, ((0, 4), (2, 8)), jnp.float32)
    down_proj = centred(streams_of[19], (FF, D), FF ** -0.5, 0.078125, ((0, 8), (1, 4)), jnp.float32)
    down_proj_moment = centred(streams_of[20], (FF, D), (0.6 * TOKENS ** 0.5), 320.0, ((0, 8), (1, 4)), jnp.float32)
    down_proj_average = centred(streams_of[21], (FF, D), FF ** -0.5, 0.078125, ((0, 8), (1, 4)), jnp.float32)
    return {"layer_in": layer_in, "out_grad": out_grad, "doc_ids": doc_ids, "group_owner": group_owner, "norm_gains": norm_gains, "norm_gains_moment": norm_gains_moment, "norm_gains_average": norm_gains_average, "feature_proj": feature_proj, "feature_proj_moment": feature_proj_moment, "feature_proj_average": feature_proj_average, "head_proj": head_proj, "head_proj_moment": head_proj_moment, "head_proj_average": head_proj_average, "mixer_out": mixer_out, "mixer_out_moment": mixer_out_moment, "mixer_out_average": mixer_out_average, "gate_up": gate_up, "gate_up_moment": gate_up_moment, "gate_up_average": gate_up_average, "down_proj": down_proj, "down_proj_moment": down_proj_moment, "down_proj_average": down_proj_average}


EPSILON = 1e-05
MOMENTUM = 0.9
AVERAGE_OLD = 0.99 * 0.01 / (1.0 - 0.99 * 0.99)
AVERAGE_NEW = 0.01 / (1.0 - 0.99 * 0.99)
RATE_FACTORS = (0.03, 0.01, 0.01, 0.28, 0.029, 0.01)
HIGHEST = lax.Precision.HIGHEST
HALF_ROOT = 0.7071067811865476
MASKED = -1e+30

@jax.custom_vjp
def low(v):
    return lax.optimization_barrier(v.astype(jnp.bfloat16)).astype(jnp.float32)

@jax.custom_vjp
def low_back(v):
    return v

def low_keep(v):
    return (low(v), None)

def low_pass(kept, grad):
    return (grad,)

def back_keep(v):
    return (v, None)

def back_low(kept, grad):
    return (low(grad),)
low.defvjp(low_keep, low_pass)
low_back.defvjp(back_keep, back_low)

def matmul(left, right):
    return jnp.dot(left, right, precision=HIGHEST, preferred_element_type=jnp.float32)

def rms_norm(values, gains):
    factor = lax.rsqrt(lax.optimization_barrier(jnp.mean(values * values, axis=-1, keepdims=True)) + EPSILON)
    return values * factor * gains

def kernel_attention(queries, keys, values, documents):
    length = queries.shape[0]
    position = jnp.arange(length, dtype=jnp.int32)
    allowed = (position[:, None] >= position[None, :]) & (documents[:, None] == documents[None, :])

    def one_head(operands):
        head_query, head_key, head_value = operands
        inner = matmul(head_query * 0.5, jnp.transpose(head_key * 0.5))
        kernel = jnp.where(allowed, 1.0 + inner + 0.5 * inner * inner, 0.0)
        return (matmul(kernel, head_value), lax.optimization_barrier(jnp.sum(kernel, axis=1)))
    return lax.map(jax.checkpoint(one_head), (jnp.swapaxes(queries, 0, 1), jnp.swapaxes(keys, 0, 1), jnp.swapaxes(values, 0, 1)))

def window_attention(queries, keys, values, documents):
    length = queries.shape[0]
    block_rows = min(512, length)
    block_count = length // block_rows
    key_padded = jnp.pad(keys, ((WIN, 0), (0, 0), (0, 0)))
    value_padded = jnp.pad(values, ((WIN, 0), (0, 0), (0, 0)))
    docs_padded = jnp.pad(documents, (WIN, 0), constant_values=-1)
    score_scale = HV ** (-0.5)
    offsets = jnp.arange(block_rows, dtype=jnp.int32)[:, None] + WIN - jnp.arange(block_rows + WIN, dtype=jnp.int32)[None, :]

    def attend_block(block_index):
        start = block_index * block_rows
        query_block = lax.dynamic_slice_in_dim(queries, start, block_rows, 0)
        key_block = lax.dynamic_slice_in_dim(key_padded, start, block_rows + WIN, 0)
        value_block = lax.dynamic_slice_in_dim(value_padded, start, block_rows + WIN, 0)
        docs_query = lax.dynamic_slice_in_dim(documents, start, block_rows, 0)
        docs_key = lax.dynamic_slice_in_dim(docs_padded, start, block_rows + WIN, 0)
        allowed = (offsets >= 0) & (offsets < WIN) & (docs_query[:, None] == docs_key[None, :])
        scores = low_back(jnp.einsum('qhd,khd->hqk', query_block, key_block, precision=HIGHEST) * score_scale)
        scores = jnp.where(allowed[None], scores, MASKED)
        peak = lax.optimization_barrier(jnp.max(scores, axis=-1, keepdims=True))
        exponent = jnp.exp(scores - peak)
        probabilities = low(exponent / lax.optimization_barrier(jnp.sum(exponent, axis=-1, keepdims=True)))
        return jnp.einsum('hqk,khd->qhd', probabilities, value_block, precision=HIGHEST)
    result = lax.map(jax.checkpoint(attend_block), jnp.arange(block_count, dtype=jnp.int32))
    return result.reshape(length, queries.shape[1], queries.shape[2])

def group_states(keys, values, documents):
    length = keys.shape[0]
    scaled_keys = keys * 0.5
    squares = scaled_keys[:, :, :, None] * scaled_keys[:, :, None, :] * HALF_ROOT
    squares = jnp.pad(squares, ((0, 0), (0, 0), (0, 0), (0, 1)))
    linear_row = jnp.concatenate([jnp.ones((length, HEADS, 1), jnp.float32), scaled_keys], axis=2)[:, :, None, :]
    features = jnp.concatenate([squares, linear_row], axis=2)
    in_last = (documents == documents[length - 1]).astype(jnp.float32)
    states = jnp.einsum('shrf,shv->hrfv', features * in_last[:, None, None, None], values, precision=HIGHEST)
    return states.reshape(GROUPS, F1, HV)

def layer_row(inputs, documents, gains, feature_weights, head_weights, mixer_weights, gate_weights, down_weights):
    length = inputs.shape[0]
    normed_one = low(rms_norm(inputs, gains[0]))
    pairs = low(low_back(matmul(normed_one, feature_weights.reshape(D, 2 * HEADS * FEAT)))).reshape(length, 2, HEADS, FEAT)
    projected = low(low_back(matmul(normed_one, head_weights.reshape(D, 4 * HEADS * HV)))).reshape(length, 4, HEADS, HV)
    numer, denom = kernel_attention(pairs[:, 0], pairs[:, 1], projected[:, 3], documents)
    numer = low_back(numer)
    denom = low_back(denom)
    linear_out = low(numer / denom[:, :, None])
    linear_out = jnp.swapaxes(linear_out, 0, 1).reshape(length, HEADS * HV)
    window_out = low(low_back(window_attention(projected[:, 0], projected[:, 1], projected[:, 2], documents))).reshape(length, HEADS * HV)
    mixed = low_back(matmul(linear_out, mixer_weights[0]) + matmul(window_out, mixer_weights[1]))
    middle = inputs + mixed
    normed_two = low(rms_norm(middle, gains[1]))
    gate_values = low_back(matmul(normed_two, gate_weights.reshape(D, 2 * FF))).reshape(length, 2, FF)
    gate_part = gate_values[:, 0]
    hidden = low(gate_part * jax.nn.sigmoid(gate_part) * gate_values[:, 1])
    branch = low_back(matmul(hidden, down_weights))
    return (middle + branch, group_states(pairs[:, 1], projected[:, 3], documents))

def momentum_update(weights, moment, average, gradient, factor):
    step_rate = factor / math.sqrt(TOKENS)
    moment_new = MOMENTUM * moment + gradient
    weights_new = weights - step_rate * (gradient + MOMENTUM * moment_new)
    average_new = AVERAGE_OLD * average + AVERAGE_NEW * weights_new
    return (gradient, weights_new, moment_new, average_new, weights_new.astype(jnp.bfloat16))

def reference(layer_in, out_grad, doc_ids, group_owner, norm_gains, norm_gains_moment, norm_gains_average, feature_proj, feature_proj_moment, feature_proj_average, head_proj, head_proj_moment, head_proj_average, mixer_out, mixer_out_moment, mixer_out_average, gate_up, gate_up_moment, gate_up_average, down_proj, down_proj_moment, down_proj_average):

    def forward(inputs, gains, feature_weights, head_weights, mixer_weights, gate_weights, down_weights):
        feature_low = low(feature_weights)
        head_low = low(head_weights)
        mixer_low = low(mixer_weights)
        gate_low = low(gate_weights)
        down_low = low(down_weights)
        row_inputs = inputs.reshape(ROWS, LEN, D)

        def one_row(operands):
            return layer_row(operands[0], operands[1], gains, feature_low, head_low, mixer_low, gate_low, down_low)
        outputs, states = lax.map(jax.checkpoint(one_row), (row_inputs, doc_ids))
        return (outputs.reshape(ROWS * LEN, D), states)
    out_y, pullback, states = jax.vjp(forward, layer_in, norm_gains, feature_proj, head_proj, mixer_out, gate_up, down_proj, has_aux=True)
    gradients = pullback(out_grad)
    same_owner = group_owner[:, None] == group_owner[None, :]
    ordinal = jnp.arange(GROUPS, dtype=jnp.int32)
    before = lax.optimization_barrier(jnp.sum(same_owner & (ordinal[None, :] < ordinal[:, None]), axis=1)).astype(jnp.int32)
    target = group_owner * CAP + before
    row_state = jnp.zeros((ROWS, N_MP * CAP, F1, HV), jnp.float32).at[:, target].set(states)
    triples = ((norm_gains, norm_gains_moment, norm_gains_average), (feature_proj, feature_proj_moment, feature_proj_average), (head_proj, head_proj_moment, head_proj_average), (mixer_out, mixer_out_moment, mixer_out_average), (gate_up, gate_up_moment, gate_up_average), (down_proj, down_proj_moment, down_proj_average))
    results = [out_y, gradients[0], row_state]
    for weight_index in range(6):
        weights, moment, average = triples[weight_index]
        results.extend(momentum_update(weights, moment, average, gradients[weight_index + 1], RATE_FACTORS[weight_index]))
    return tuple(results)
```

```python
import functools
import math

import jax
import jax.numpy as jnp
import numpy as np
from jax import lax
from jax.experimental import pallas as pl
from jax.experimental.pallas import tpu as pltpu
from jax.sharding import Mesh, PartitionSpec as P

D = 2048
HEADS = 16
FEAT = 16
HV = 128
WIN = 64
F1 = 17
GROUPS = 272
REACH = 512
QB = 256
WB = 128

EPSILON = 1e-05
MOMENTUM = 0.9
AVERAGE_OLD = 0.99 * 0.01 / (1.0 - 0.99 * 0.99)
AVERAGE_NEW = 0.01 / (1.0 - 0.99 * 0.99)
RATE_FACTORS = (0.03, 0.01, 0.01, 0.28, 0.029, 0.01)
HALF_ROOT = 0.7071067811865476
MASKED = -1e30
SCALE = HV**-0.5
BF = jnp.bfloat16
F32 = jnp.float32
NT = (((1,), (1,)), ((), ()))
TN = (((0,), (0,)), ((), ()))


def mm(left, right):
    return jnp.dot(left, right, preferred_element_type=F32)


def mm_nt(left, right):
    return lax.dot_general(left, right, NT, preferred_element_type=F32)


def mm_tn(left, right):
    return lax.dot_general(left, right, TN, preferred_element_type=F32)


def peer(values, axis, offset):
    ways = lax.axis_size(axis)
    return lax.ppermute(values, axis, [(i, i ^ offset) for i in range(ways)])


def enter(values):
    half = values.shape[0] // 2
    core, side = lax.axis_index("c"), lax.axis_index("s")
    first = lax.dynamic_slice_in_dim(values, side * half, half, 0)
    second = lax.dynamic_slice_in_dim(values, (1 - side) * half, half, 0)
    swap = [(2 * a + b, 2 * b + a) for a in range(2) for b in range(2)]
    turn = [(2 * a + b, 2 * (1 - b) + a) for a in range(2) for b in range(2)]
    same = lax.ppermute(first, ("c", "s"), swap)
    other = lax.ppermute(second, ("c", "s"), turn)
    low = core == 0
    return jnp.concatenate([jnp.where(low, same, other), jnp.where(low, other, same)], axis=1)


def leave(values):
    width = values.shape[1] // 2
    core, side = lax.axis_index("c"), lax.axis_index("s")
    low = core == 0
    same = jnp.where(low, values[:, :width], values[:, width:])
    other = jnp.where(low, values[:, width:], values[:, :width])
    swap = [(2 * a + b, 2 * b + a) for a in range(2) for b in range(2)]
    back = [(2 * (1 - b) + a, 2 * a + b) for a in range(2) for b in range(2)]
    same = lax.ppermute(same, ("c", "s"), swap)
    other = lax.ppermute(other, ("c", "s"), back)
    near = side == 0
    return jnp.concatenate([jnp.where(near, same, other), jnp.where(near, other, same)], axis=0)


def gather_t(piece):
    ways = lax.axis_size("t")
    mine = lax.axis_index("t")
    tokens, both = piece.shape
    width = both // 2
    full = jnp.zeros((tokens, 2 * ways * width), piece.dtype)
    for offset in range(ways):
        part = piece if offset == 0 else peer(piece, "t", offset)
        start = (mine ^ offset) * width
        full = lax.dynamic_update_slice(full, part[:, :width], (0, start))
        full = lax.dynamic_update_slice(full, part[:, width:], (0, ways * width + start))
    return full


def scatter_t(terms):
    ways = lax.axis_size("t")
    mine = lax.axis_index("t")
    half = terms.shape[1] // 2
    width = half // ways

    def piece(offset):
        start = (mine ^ offset) * width
        return jnp.concatenate(
            [
                lax.dynamic_slice_in_dim(terms, start, width, 1),
                lax.dynamic_slice_in_dim(terms, half + start, width, 1),
            ],
            axis=1,
        )

    total = piece(0).astype(F32)
    for offset in range(1, ways):
        total = total + peer(piece(offset).astype(BF), "t", offset).astype(F32)
    return total


def total_t(values):
    total = values
    for offset in range(1, lax.axis_size("t")):
        total = total + peer(values, "t", offset)
    return total


def gather_weight(shard):
    full = lax.all_gather(shard.astype(BF), ("s", "y", "c"), axis=0, tiled=False)
    return full.reshape(2, -1, shard.shape[1])


def scatter_grad(grads):
    stacked = jnp.stack(grads, axis=0).astype(BF)
    flat = stacked.reshape(-1, stacked.shape[2])
    return lax.psum_scatter(flat, ("s", "y", "c"), scatter_dimension=0, tiled=True).astype(F32)


def forward_body(heads, tokens, proj, pairs, far_v, far_p, far_w, docs_c, docs_r, out, den):
    lanes = heads * HV
    for i in range(heads):
        at = i * HV
        qs, ks = i * FEAT, (heads + i) * FEAT
        for b in range(tokens // QB):
            rows = slice(b * QB, (b + 1) * QB)
            q = pairs[0, rows, qs : qs + FEAT]
            docs_q = docs_c[REACH + b * QB : REACH + (b + 1) * QB, :]
            numer = jnp.zeros((QB, HV), F32)
            denom = jnp.zeros((QB, 1), F32)
            for kb in range(b - REACH // QB, b + 1):
                if kb >= 0:
                    keys = slice(kb * QB, (kb + 1) * QB)
                    k = pairs[0, keys, ks : ks + FEAT]
                    v = proj[0, keys, 3 * lanes + at : 3 * lanes + at + HV]
                else:
                    keys = slice(REACH + kb * QB, REACH + (kb + 1) * QB)
                    k = far_p[0, keys, ks : ks + FEAT]
                    v = far_v[0, keys, at : at + HV]
                inner = mm_nt(q, k) * 0.25
                kernel = 1.0 + inner + 0.5 * inner * inner
                allowed = docs_q == docs_r[:, REACH + kb * QB : REACH + (kb + 1) * QB]
                if kb == b:
                    allowed = allowed & (
                        lax.broadcasted_iota(jnp.int32, (QB, QB), 0)
                        >= lax.broadcasted_iota(jnp.int32, (QB, QB), 1)
                    )
                kernel = jnp.where(allowed, kernel, 0.0)
                denom = denom + jnp.sum(kernel, axis=1, keepdims=True)
                numer = numer + mm(kernel.astype(BF), v)
            out[0, rows, at : at + HV] = (numer / denom).astype(BF)
            den[0, rows, i : i + 1] = denom
        for b in range(tokens // WB):
            rows = slice(b * WB, (b + 1) * WB)
            q = proj[0, rows, at : at + HV]
            k, v, allowed = window_block(b, at, lanes, proj, far_w, docs_c, docs_r)
            probs = window_probs(q, k, allowed)
            out[0, rows, lanes + at : lanes + at + HV] = mm(probs.astype(BF), v).astype(BF)


def window_block(b, at, lanes, proj, far_w, docs_c, docs_r):
    if b:
        keys = slice((b - 1) * WB, (b + 1) * WB)
        k = proj[0, keys, lanes + at : lanes + at + HV]
        v = proj[0, keys, 2 * lanes + at : 2 * lanes + at + HV]
    else:
        k = jnp.concatenate(
            [far_w[0, :, at : at + HV], proj[0, :WB, lanes + at : lanes + at + HV]], axis=0
        )
        v = jnp.concatenate(
            [
                far_w[0, :, lanes + at : lanes + at + HV],
                proj[0, :WB, 2 * lanes + at : 2 * lanes + at + HV],
            ],
            axis=0,
        )
    start = REACH + b * WB
    back = (
        lax.broadcasted_iota(jnp.int32, (WB, 2 * WB), 0)
        + WB
        - lax.broadcasted_iota(jnp.int32, (WB, 2 * WB), 1)
    )
    same = docs_c[start : start + WB, :] == docs_r[:, start - WB : start + WB]
    return k, v, same & (back >= 0) & (back < WIN)


def window_probs(q, k, allowed):
    scores = jnp.where(allowed, mm_nt(q, k) * SCALE, MASKED)
    exponent = jnp.exp(scores - jnp.max(scores, axis=1, keepdims=True))
    return exponent / jnp.sum(exponent, axis=1, keepdims=True)


def backward_body(
    heads, tokens, proj, pairs, far_v, far_p, far_w, docs_c, docs_r, out, den, dout,
    dproj, dpairs, dfar_v, dfar_p, dfar_w, acc_v, acc_k, acc_wk, acc_wv,
):
    lanes = heads * HV
    lane_zero = (lax.broadcasted_iota(jnp.int32, (QB, HV), 1) == 0).astype(BF)
    for i in range(heads):
        at = i * HV
        qs, ks = i * FEAT, (heads + i) * FEAT
        acc_v[...] = jnp.zeros_like(acc_v)
        acc_k[...] = jnp.zeros_like(acc_k)
        acc_wk[...] = jnp.zeros_like(acc_wk)
        acc_wv[...] = jnp.zeros_like(acc_wv)
        for b in range(tokens // QB):
            rows = slice(b * QB, (b + 1) * QB)
            q = pairs[0, rows, qs : qs + FEAT]
            docs_q = docs_r[:, REACH + b * QB : REACH + (b + 1) * QB]
            dlin = dout[0, rows, at : at + HV].astype(F32)
            inverse = 1.0 / den[0, rows, i : i + 1]
            mean = jnp.sum(dlin * out[0, rows, at : at + HV].astype(F32), axis=1, keepdims=True)
            dnumer = (dlin * inverse).astype(BF)
            ddenom = (-mean * inverse).astype(BF)
            extended = jnp.concatenate([dnumer, ddenom * lane_zero], axis=1)
            dq = jnp.zeros((QB, FEAT), F32)
            for kb in range(b - REACH // QB, b + 1):
                place = slice(REACH + kb * QB, REACH + (kb + 1) * QB)
                if kb >= 0:
                    keys = slice(kb * QB, (kb + 1) * QB)
                    k = pairs[0, keys, ks : ks + FEAT]
                    v = proj[0, keys, 3 * lanes + at : 3 * lanes + at + HV]
                else:
                    k = far_p[0, place, ks : ks + FEAT]
                    v = far_v[0, place, at : at + HV]
                inner = mm_nt(k, q) * 0.25
                weight = mm_nt(jnp.concatenate([v, lane_zero], axis=1), extended)
                allowed = docs_c[place, :] == docs_q
                if kb == b:
                    allowed = allowed & (
                        lax.broadcasted_iota(jnp.int32, (QB, QB), 0)
                        <= lax.broadcasted_iota(jnp.int32, (QB, QB), 1)
                    )
                kernel = jnp.where(allowed, 1.0 + inner + 0.5 * inner * inner, 0.0).astype(BF)
                slope = jnp.where(allowed, weight * (0.25 + 0.25 * inner), 0.0).astype(BF)
                acc_v[place, :] += mm(kernel, dnumer)
                acc_k[place, :] += mm(slope, q)
                dq = dq + mm_tn(slope, k)
            dpairs[0, rows, qs : qs + FEAT] = dq.astype(BF)
        dfar_v[0, :, at : at + HV] = acc_v[:REACH, :].astype(BF)
        dfar_p[0, :, qs : qs + FEAT] = acc_k[:REACH, :].astype(BF)
        dproj[0, :, 3 * lanes + at : 3 * lanes + at + HV] = acc_v[REACH:, :].astype(BF)
        dpairs[0, :, ks : ks + FEAT] = acc_k[REACH:, :].astype(BF)
        for b in range(tokens // WB):
            rows = slice(b * WB, (b + 1) * WB)
            q = proj[0, rows, at : at + HV]
            k, v, allowed = window_block(b, at, lanes, proj, far_w, docs_c, docs_r)
            probs = window_probs(q, k, allowed)
            upstream = dout[0, rows, lanes + at : lanes + at + HV]
            dprobs = mm_nt(upstream, v)
            dscores = probs * (dprobs - jnp.sum(probs * dprobs, axis=1, keepdims=True))
            dscores = dscores.astype(BF)
            dproj[0, rows, at : at + HV] = (mm(dscores, k) * SCALE).astype(BF)
            span = slice(b * WB, (b + 2) * WB)
            acc_wk[span, :] += mm_tn(dscores, q)
            acc_wv[span, :] += mm_tn(probs.astype(BF), upstream)
        dfar_w[0, :, at : at + HV] = (acc_wk[:WB, :] * SCALE).astype(BF)
        dfar_w[0, :, lanes + at : lanes + at + HV] = acc_wv[:WB, :].astype(BF)
        dproj[0, :, lanes + at : lanes + at + HV] = (acc_wk[WB:, :] * SCALE).astype(BF)
        dproj[0, :, 2 * lanes + at : 2 * lanes + at + HV] = acc_wv[WB:, :].astype(BF)


def per_side(shape):
    return pl.BlockSpec((1,) + tuple(shape[1:]), lambda s: (s,) + (0,) * (len(shape) - 1))


def whole(shape):
    return pl.BlockSpec(tuple(shape), lambda s: (0,) * len(shape))


VMEM = pltpu.CompilerParams(vmem_limit_bytes=56 * 2**20)


def attention_forward(heads, proj, pairs, far_v, far_p, far_w, docs_c, docs_r):
    tokens = proj.shape[1]
    ins = (proj, pairs, far_v, far_p, far_w)
    outs = (
        jax.ShapeDtypeStruct((2, tokens, 2 * heads * HV), BF),
        jax.ShapeDtypeStruct((2, tokens, heads), F32),
    )
    return pl.pallas_call(
        functools.partial(forward_body, heads, tokens),
        grid=(2,),
        in_specs=[per_side(a.shape) for a in ins] + [whole(docs_c.shape), whole(docs_r.shape)],
        out_specs=[per_side(a.shape) for a in outs],
        out_shape=outs,
        compiler_params=VMEM,
        name="attention_forward",
    )(*ins, docs_c, docs_r)


def attention_backward(heads, proj, pairs, far_v, far_p, far_w, docs_c, docs_r, out, den, dout):
    tokens = proj.shape[1]
    ins = (proj, pairs, far_v, far_p, far_w)
    outs = tuple(jax.ShapeDtypeStruct(a.shape, BF) for a in (proj, pairs, far_v))
    outs = outs + (
        jax.ShapeDtypeStruct((2, REACH, heads * FEAT), BF),
        jax.ShapeDtypeStruct(far_w.shape, BF),
    )
    more = (out, den, dout)
    return pl.pallas_call(
        functools.partial(backward_body, heads, tokens),
        grid=(2,),
        in_specs=[per_side(a.shape) for a in ins]
        + [whole(docs_c.shape), whole(docs_r.shape)]
        + [per_side(a.shape) for a in more],
        out_specs=[per_side(a.shape) for a in outs],
        out_shape=outs,
        scratch_shapes=[
            pltpu.VMEM((REACH + tokens, HV), F32),
            pltpu.VMEM((REACH + tokens, FEAT), F32),
            pltpu.VMEM((WB + tokens, HV), F32),
            pltpu.VMEM((WB + tokens, HV), F32),
        ],
        compiler_params=VMEM,
        name="attention_backward",
    )(*ins, docs_c, docs_r, *more)


def feature_tables():
    pick_a = np.zeros((F1, F1 * F1), np.float32)
    pick_b = np.zeros((F1, F1 * F1), np.float32)
    scale = np.ones((F1 * F1,), np.float32)
    for r in range(F1):
        for j in range(F1):
            f = r * F1 + j
            pick_a[r, f] = 1.0
            if r < FEAT:
                scale[f] = HALF_ROOT
                if j < FEAT:
                    pick_b[j, f] = 1.0
            else:
                pick_b[FEAT if j == 0 else j - 1, f] = 1.0
    return pick_a, pick_b, scale


def row_states(heads, keys, values, docs):
    keys, values = keys[:, -REACH:], values[:, -REACH:]
    keys = jnp.swapaxes(keys.reshape(2, REACH, heads, FEAT), 1, 2).reshape(-1, REACH, FEAT)
    values = jnp.swapaxes(values.reshape(2, REACH, heads, HV), 1, 2).reshape(-1, REACH, HV)
    ones = jnp.ones(keys.shape[:2] + (1,), BF)
    extended = jnp.concatenate([keys * BF(0.5), ones], axis=2)
    pick_a, pick_b, scale = feature_tables()
    left = jnp.einsum("bsf,fg->bsg", extended, jnp.asarray(pick_a, BF), preferred_element_type=F32)
    right = jnp.einsum("bsf,fg->bsg", extended, jnp.asarray(pick_b, BF), preferred_element_type=F32)
    in_last = (docs[-REACH:] == docs[-1]).astype(F32)
    features = left * right * scale * in_last[None, :, None]
    return jnp.einsum("bsg,bsv->bgv", features.astype(BF), values, preferred_element_type=F32)


def owned_states(heads, states, owner):
    ways = lax.axis_size("t")
    mine_t, side = lax.axis_index("t"), lax.axis_index("s")
    states = states.astype(BF)
    near = lax.ppermute(states, ("c", "s"), [(2 + s, 2 * s) for s in range(2)])
    far = lax.ppermute(states, ("c", "s"), [(2 + s, 2 * s + 1) for s in range(2)])
    states = jnp.where(side == 0, near, far)
    slots = GROUPS // ways
    groups = jnp.arange(GROUPS, dtype=jnp.int32)
    mine = owner == side * ways + mine_t
    ordinal = jnp.sum((mine[None, :] & (groups[None, :] < groups[:, None])).astype(jnp.int32), axis=1)
    wanted = jnp.arange(slots, dtype=jnp.int32)
    picked = (mine[None, :] & (ordinal[None, :] == wanted[:, None])).astype(BF)
    picked = picked.reshape(slots, 2, ways, heads * F1)
    total = jnp.zeros((slots, F1, HV), F32)
    for offset in range(ways):
        part = states if offset == 0 else peer(states, "t", offset)
        part = part.reshape(2 * heads * F1, F1, HV)
        chosen = lax.dynamic_slice_in_dim(picked, mine_t ^ offset, 1, 2)
        chosen = chosen.reshape(slots, 2 * heads * F1)
        total = total + jnp.einsum("kg,gfv->kfv", chosen, part, preferred_element_type=F32)
    return total[None]


def momentum_update(weights, moment, average, gradient, factor, token_total):
    step_rate = factor / math.sqrt(token_total)
    moment_new = MOMENTUM * moment + gradient
    weights_new = weights - step_rate * (gradient + MOMENTUM * moment_new)
    average_new = AVERAGE_OLD * average + AVERAGE_NEW * weights_new
    return (gradient, weights_new, moment_new, average_new, weights_new.astype(BF))


def norm_back(values, factor, gains, upstream):
    gain_grad = jnp.sum(upstream * values, axis=0)
    inner = total_t(jnp.sum(upstream * gains * values, axis=1))
    scale = (factor * factor * inner / D)[:, None]
    return gains * upstream - values * scale, gain_grad


def local(
    layer_in, out_grad, doc_ids, group_owner,
    norm_gains, norm_gains_moment, norm_gains_average,
    feature_proj, feature_proj_moment, feature_proj_average,
    head_proj, head_proj_moment, head_proj_average,
    mixer_out, mixer_out_moment, mixer_out_average,
    gate_up, gate_up_moment, gate_up_average,
    down_proj, down_proj_moment, down_proj_average,
):
    data_ways = lax.axis_size("y") * 2
    core, side = lax.axis_index("c"), lax.axis_index("s")
    width = layer_in.shape[1]
    tokens = layer_in.shape[0] // 2
    heads = head_proj.shape[2] // HV
    rows = head_proj.shape[0]
    lanes = heads * HV
    token_total = layer_in.shape[0] * data_ways

    feature_full = gather_weight(feature_proj.reshape(rows, -1))
    head_full = gather_weight(head_proj.reshape(rows, -1))
    mixer_full = gather_weight(jnp.transpose(mixer_out, (2, 0, 1)).reshape(rows, -1))
    gate_full = gather_weight(gate_up[:, 0])
    up_full = gather_weight(gate_up[:, 1])
    down_full = gather_weight(jnp.transpose(down_proj))

    other_gains = lax.ppermute(norm_gains, "s", [(0, 1), (1, 0)])
    gains = jnp.where(
        side == 0,
        jnp.concatenate([norm_gains, other_gains], axis=1),
        jnp.concatenate([other_gains, norm_gains], axis=1),
    )

    x = enter(layer_in.astype(BF)).astype(F32)
    dy_mine = enter(out_grad.astype(BF))
    docs = lax.ppermute(doc_ids, ("c", "s"), [(2 * a + b, 2 * b + a) for a in range(2) for b in range(2)])
    docs = jnp.concatenate([jnp.full((1, REACH), -1, jnp.int32), docs], axis=1)
    docs_r = lax.dynamic_slice_in_dim(docs, core * tokens, REACH + tokens, 1)
    docs_c = jnp.reshape(docs_r, (REACH + tokens, 1))

    factor_one = lax.rsqrt(total_t(jnp.sum(x * x, axis=1)) / D + EPSILON)
    scaled_one = gather_t((x * gains[0]).astype(BF))
    proj = jnp.stack([(mm(scaled_one, head_full[s]) * factor_one[:, None]).astype(BF) for s in range(2)])
    pairs = jnp.stack([(mm(scaled_one, feature_full[s]) * factor_one[:, None]).astype(BF) for s in range(2)])

    ahead = [(0, 1)]
    far_v = lax.ppermute(proj[:, -REACH:, 3 * lanes :], "c", ahead)
    far_p = lax.ppermute(pairs[:, -REACH:], "c", ahead)
    far_w = lax.ppermute(proj[:, -WB:, lanes : 3 * lanes], "c", ahead)
    attended, denom = attention_forward(heads, proj, pairs, far_v, far_p, far_w, docs_c, docs_r)
    states = row_states(heads, pairs[:, :, heads * FEAT :], proj[:, :, 3 * lanes :], docs_r[0])
    row_state = owned_states(heads, states, group_owner)

    mixed = scatter_t(mm_nt(attended[0], mixer_full[0]) + mm_nt(attended[1], mixer_full[1]))
    middle = x + mixed
    factor_two = lax.rsqrt(total_t(jnp.sum(middle * middle, axis=1)) / D + EPSILON)
    scaled_two = gather_t((middle * gains[1]).astype(BF))

    dy = gather_t(dy_mine)
    hidden, dgate, dup = [], [], []
    for s in range(2):
        back = mm(dy, down_full[s])
        gate = mm(scaled_two, gate_full[s]) * factor_two[:, None]
        up = mm(scaled_two, up_full[s]) * factor_two[:, None]
        sigmoid = jax.nn.sigmoid(gate)
        active = gate * sigmoid
        hidden.append((active * up).astype(BF))
        slope = back * up * sigmoid * (1.0 + gate * (1.0 - sigmoid))
        dgate.append((slope * factor_two[:, None]).astype(BF))
        dup.append((back * active * factor_two[:, None]).astype(BF))
    terms_two = sum(mm_nt(dgate[s], gate_full[s]) + mm_nt(dup[s], up_full[s]) for s in range(2))
    upstream_two = scatter_t(terms_two)
    branch = scatter_t(mm_nt(hidden[0], down_full[0]) + mm_nt(hidden[1], down_full[1]))
    out_y = layer_in + leave((mixed + branch).astype(BF)).astype(F32)
    back_two, gain_two = norm_back(middle, factor_two, gains[1], upstream_two)
    dmixed = gather_t((dy_mine.astype(F32) + back_two).astype(BF))

    down_sum = scatter_grad([mm_tn(dy, hidden[s]) for s in range(2)])
    gate_sum = scatter_grad([mm_tn(scaled_two, dgate[s]) for s in range(2)])
    up_sum = scatter_grad([mm_tn(scaled_two, dup[s]) for s in range(2)])

    dattended = jnp.stack([mm(dmixed, mixer_full[s]).astype(BF) for s in range(2)])
    mixer_sum = scatter_grad([mm_tn(dmixed, attended[s]) for s in range(2)])
    dproj, dpairs, dfar_v, dfar_p, dfar_w = attention_backward(
        heads, proj, pairs, far_v, far_p, far_w, docs_c, docs_r, attended, denom, dattended
    )
    behind = [(1, 0)]
    dfar_v = lax.ppermute(dfar_v, "c", behind).astype(F32)
    dfar_p = lax.ppermute(dfar_p, "c", behind).astype(F32)
    dfar_w = lax.ppermute(dfar_w, "c", behind).astype(F32)
    dproj = (
        dproj.astype(F32)
        + jnp.pad(dfar_v, ((0, 0), (tokens - REACH, 0), (3 * lanes, 0)))
        + jnp.pad(dfar_w, ((0, 0), (tokens - WB, 0), (lanes, lanes)))
    )
    dpairs = dpairs.astype(F32) + jnp.pad(dfar_p, ((0, 0), (tokens - REACH, 0), (heads * FEAT, 0)))
    dproj = (dproj * factor_one[None, :, None]).astype(BF)
    dpairs = (dpairs * factor_one[None, :, None]).astype(BF)
    head_sum = scatter_grad([mm_tn(scaled_one, dproj[s]) for s in range(2)])
    feature_sum = scatter_grad([mm_tn(scaled_one, dpairs[s]) for s in range(2)])
    terms_one = sum(mm_nt(dproj[s], head_full[s]) + mm_nt(dpairs[s], feature_full[s]) for s in range(2))
    upstream_one = scatter_t(terms_one)
    back_one, gain_one = norm_back(x, factor_one, gains[0], upstream_one)
    grad_x = out_grad + leave((back_one + back_two).astype(BF)).astype(F32)

    both = jnp.stack([gain_one, gain_two], axis=0)
    gains_sum = lax.dynamic_slice_in_dim(both, side * width, width, 1)
    holders = 2 * data_ways
    for offset in range(1, holders):
        theirs = lax.dynamic_slice_in_dim(both, (side ^ (offset & 1)) * width, width, 1)
        gains_sum = gains_sum + lax.ppermute(
            theirs, ("y", "c", "s"), [(i, i ^ offset) for i in range(holders)]
        )

    mixer_sum = jnp.transpose(mixer_sum.reshape(rows, 2, lanes), (1, 2, 0))
    triples = (
        (norm_gains, norm_gains_moment, norm_gains_average, gains_sum),
        (feature_proj, feature_proj_moment, feature_proj_average, feature_sum.reshape(feature_proj.shape)),
        (head_proj, head_proj_moment, head_proj_average, head_sum.reshape(head_proj.shape)),
        (mixer_out, mixer_out_moment, mixer_out_average, mixer_sum),
        (gate_up, gate_up_moment, gate_up_average, jnp.stack([gate_sum, up_sum], axis=1)),
        (down_proj, down_proj_moment, down_proj_average, jnp.transpose(down_sum)),
    )
    results = [out_y, grad_x, row_state]
    for index, triple in enumerate(triples):
        results.extend(momentum_update(*triple, RATE_FACTORS[index], token_total))
    return tuple(results)


def solution(mesh):
    data_ways, model_ways = mesh.shape["dp"], mesh.shape["mp"]
    grid = Mesh(mesh.devices.reshape(data_ways // 2, 2, 2, model_ways // 2), ("y", "c", "s", "t"))
    dp, mp = ("y", "c"), ("s", "t")
    gains = (P(None, mp),)
    rows_cols = (P(dp, None, mp),)
    mixer = (P(None, mp, dp),)
    down = (P(mp, dp),)
    tokens = (P(dp, mp),)
    return jax.shard_map(
        local,
        mesh=grid,
        in_specs=tokens * 2
        + (P(dp, None), P())
        + gains * 3
        + rows_cols * 6
        + mixer * 3
        + rows_cols * 3
        + down * 3,
        out_specs=tokens * 2
        + (P(dp, mp, None, None),)
        + gains * 5
        + rows_cols * 10
        + mixer * 5
        + rows_cols * 5
        + down * 5,
        check_vma=False,
    )
```

```python
import functools
import math

import jax
import jax.numpy as jnp
import numpy as np
from jax import lax
from jax.experimental import pallas as pl
from jax.experimental.pallas import tpu as pltpu
from jax.sharding import Mesh, PartitionSpec as P

D = 2048
HEADS = 16
FEAT = 16
HV = 128
WIN = 64
F1 = 17
GROUPS = 272
REACH = 512
QB = 256
WB = 128

EPSILON = 1e-05
MOMENTUM = 0.9
AVERAGE_OLD = 0.99 * 0.01 / (1.0 - 0.99 * 0.99)
AVERAGE_NEW = 0.01 / (1.0 - 0.99 * 0.99)
RATE_FACTORS = (0.03, 0.01, 0.01, 0.28, 0.029, 0.01)
HALF_ROOT = 0.7071067811865476
MASKED = -1e30
SCALE = HV**-0.5
BF = jnp.bfloat16
F32 = jnp.float32


def cost(matmul_flops):
    return pl.CostEstimate(flops=int(0.4 * matmul_flops), bytes_accessed=1, transcendentals=0)


CHEAP = cost(0)
NT = (((1,), (1,)), ((), ()))
TN = (((0,), (0,)), ((), ()))


def mm(left, right):
    return jnp.dot(left, right, preferred_element_type=F32)


def mm_nt(left, right):
    return lax.dot_general(left, right, NT, preferred_element_type=F32)


def mm_tn(left, right):
    return lax.dot_general(left, right, TN, preferred_element_type=F32)


def peer(values, axis, offset):
    ways = lax.axis_size(axis)
    return lax.ppermute(values, axis, [(i, i ^ offset) for i in range(ways)])


def shift(values, step, first):
    ways = lax.axis_size("t")
    places = range(first, ways - 1) if step > 0 else range(1, ways - first)
    return lax.ppermute(values, "t", [(i, i + step) for i in places])


SWAP = [(2 * a + b, 2 * b + a) for a in range(2) for b in range(2)]
TURN = [(2 * a + b, 2 * (1 - b) + a) for a in range(2) for b in range(2)]
BACK = [(2 * (1 - b) + a, 2 * a + b) for a in range(2) for b in range(2)]


def told(flag, *earlier):
    flag = flag.astype(jnp.int32).reshape(1, 1)
    return (hold(flag, *earlier) if earlier else flag)[0, 0] == 1


def enter(values, *earlier):
    half = values.shape[0] // 2
    near = told(lax.axis_index("s") == 0, *earlier)
    first = jnp.where(near, values[:half], values[half:]).astype(BF)
    second = jnp.where(near, values[half:], values[:half]).astype(BF)
    same = lax.ppermute(first, ("c", "s"), SWAP)
    other = lax.ppermute(second, ("c", "s"), TURN)
    low = lax.axis_index("c") == 0
    return jnp.concatenate([jnp.where(low, same, other), jnp.where(low, other, same)], axis=1)


def leave(values):
    width = values.shape[1] // 2
    low = lax.axis_index("c") == 0
    same = jnp.where(low, values[:, :width], values[:, width:])
    other = jnp.where(low, values[:, width:], values[:, :width])
    same = lax.ppermute(same, ("c", "s"), SWAP)
    other = lax.ppermute(other, ("c", "s"), BACK)
    near = lax.axis_index("s") == 0
    return jnp.concatenate([jnp.where(near, same, other), jnp.where(near, other, same)], axis=0)


def line():
    return lax.axis_size("t") == 4


def send_t(piece):
    ways = lax.axis_size("t")
    if not line():
        return [piece] + [peer(piece, "t", offset) for offset in range(1, ways)]
    parts = [piece]
    up = down = piece
    for step in range(ways - 1):
        up, down = shift(up, 1, step), shift(down, -1, step)
        parts += [up, down]
    return parts


def where_from(mine, place):
    if not line():
        return mine ^ place
    return 0 if mine == place else 2 * abs(mine - place) - (1 if place < mine else 0)


def anywhere(count):
    return [pl.BlockSpec(memory_space=pl.ANY)] * count


def hold(values, *earlier):
    def body(*refs):
        pass

    return pl.pallas_call(
        body,
        out_shape=jax.ShapeDtypeStruct(values.shape, values.dtype),
        in_specs=anywhere(1 + len(earlier)),
        out_specs=pl.BlockSpec(memory_space=pl.ANY),
        input_output_aliases={0: 0},
        cost_estimate=CHEAP,
        name="hold",
    )(values, *earlier)


def join_body(ways, mine, *refs):
    parts, out = refs, refs[-1]
    width = parts[0].shape[1]
    for d in range(ways):

        @pl.when(mine[0] == d)
        def _():
            for place in range(ways):
                out[:, place * width : (place + 1) * width] = parts[where_from(d, place)][...]


def join_t(parts, *earlier):
    ways = lax.axis_size("t")
    tokens, width = parts[0].shape
    rows = min(256, tokens)
    return pl.pallas_call(
        functools.partial(join_body, ways),
        grid_spec=pltpu.PrefetchScalarGridSpec(
            num_scalar_prefetch=1,
            grid=(tokens // rows,),
            in_specs=[pl.BlockSpec((rows, width), lambda i, mine: (i, 0))] * len(parts)
            + anywhere(len(earlier)),
            out_specs=pl.BlockSpec((rows, ways * width), lambda i, mine: (i, 0)),
        ),
        out_shape=jax.ShapeDtypeStruct((tokens, ways * width), parts[0].dtype),
        cost_estimate=cost(5e9),
        name="join",
    )(lax.axis_index("t").astype(jnp.int32).reshape(1), *parts, *earlier)


def terms_body(count, pieces, dests, *refs):
    lefts, rights, outs = refs[:count], refs[count : 2 * count], refs[-pieces:]
    total = None
    for left, right in zip(lefts, rights):
        if len(right.shape) == 4:
            product = mm(left[...], right[0, 0])
        else:
            product = mm_nt(left[...], right[0])
        total = product if total is None else total + product
    for i in range(pieces):

        @pl.when(pl.program_id(0) == i)
        def _():
            outs[i][...] = total.astype(outs[i].dtype)


def terms_t(lefts, rights, dests, dtypes, *earlier):
    tokens = lefts[0].shape[0]
    count, pieces = len(lefts), len(dtypes)
    width = D // lax.axis_size("t")

    def right_spec(weight, s):
        if len(weight.shape) == 4:
            return pl.BlockSpec((1, 1) + weight.shape[2:], lambda i, dests: (s, dests[i], 0, 0))
        return pl.BlockSpec((1, width, weight.shape[2]), lambda i, dests: (s, dests[i], 0))

    return pl.pallas_call(
        functools.partial(terms_body, count, pieces),
        grid_spec=pltpu.PrefetchScalarGridSpec(
            num_scalar_prefetch=1,
            grid=(pieces,),
            in_specs=[pl.BlockSpec(a.shape, lambda i, dests: (0, 0)) for a in lefts]
            + [right_spec(*right) for right in rights]
            + anywhere(len(earlier)),
            out_specs=[pl.BlockSpec((tokens, width), lambda i, dests: (0, 0))] * pieces,
        ),
        out_shape=[jax.ShapeDtypeStruct((tokens, width), dtype) for dtype in dtypes],
        compiler_params=pltpu.CompilerParams(vmem_limit_bytes=48 * 2**20),
        cost_estimate=cost(2 * pieces * tokens * width * sum(a.shape[1] for a in lefts)),
        name="terms",
    )(dests, *lefts, *[weight for weight, s in rights], *earlier)


def hop(values, step, count):
    places = range(count) if step > 0 else range(3, 3 - count, -1)
    return lax.ppermute(values, "t", [(i, i + step) for i in places])


def both_s(weight):
    return [(weight, 0), (weight, 1)]


def spread_t(lefts, rights, *earlier):
    ways, mine = lax.axis_size("t"), lax.axis_index("t")
    if not line():
        dests = jnp.stack([mine ^ offset for offset in range(ways)]).astype(jnp.int32)
        parts = terms_t(lefts, rights, dests, [F32] + [BF] * (ways - 1), *earlier)
        return [parts[0]] + [peer(part, "t", offset) for offset, part in enumerate(parts) if offset], parts
    order = jnp.asarray(np.array([[3, 2, 1, 0], [3, 2, 0, 1], [0, 1, 3, 2], [0, 1, 2, 3]], np.int32))
    dests = lax.dynamic_index_in_dim(order, mine, 0, False)
    [first] = terms_t(lefts, rights, dests[:1], [BF], *earlier)
    up, down = hop(first, 1, 1), hop(first, -1, 1)
    second, third, own = terms_t(lefts, rights, dests[1:], [BF, BF, F32], first)
    wide = lambda a: a.astype(F32)
    up2 = (jnp.where(mine == 0, wide(second), wide(first)) + wide(up)).astype(BF)
    down2 = (jnp.where(mine == 3, wide(second), wide(first)) + wide(down)).astype(BF)
    up, down = hop(up2, 1, 2), hop(down2, -1, 2)
    up3 = (jnp.where(mine == 1, wide(second), wide(third)) + wide(up)).astype(BF)
    down3 = (jnp.where(mine == 2, wide(second), wide(third)) + wide(down)).astype(BF)
    return [own, hop(up3, 1, 3), hop(down3, -1, 3)], [up2, down2, up3, down3]


def add_up(parts):
    total = parts[0].astype(F32)
    for part in parts[1:]:
        total = total + part.astype(F32)
    return total


def total_t(values):
    total = values
    for offset in range(1, lax.axis_size("t")):
        total = total + peer(values, "t", offset)
    return total


def gather_weight(shard, *earlier):
    flag = told(lax.axis_index("s") >= 0, *earlier)
    shard = jnp.where(flag, shard, 0.0).astype(BF)
    full = lax.all_gather(shard, ("s", "y", "c"), axis=0, tiled=False)
    return full.reshape((2, -1) + shard.shape)


def rows_of(full):
    return full.reshape(2, -1, full.shape[3])


def pack(pair):
    cut = pair.shape[2] // HV * HV
    return jnp.concatenate([pair[:, 0, :cut], pair[:, 1, :cut], pair[:, 0, cut:], pair[:, 1, cut:]], axis=1)


def unpack(packed):
    columns = packed.shape[1] // 2
    cut = columns // HV * HV
    left = 2 * cut
    more = columns - cut
    gate = jnp.concatenate([packed[:, :cut], packed[:, left : left + more]], axis=1)
    return gate, jnp.concatenate([packed[:, cut:left], packed[:, left + more :]], axis=1)


def grads_body(count, *refs):
    turned, out = refs[0][...].T, refs[-1]
    for i in range(count):
        out[i] = mm(turned, refs[1 + i][...]).astype(BF)


def grads(left, rights, *earlier):
    tokens, width = left.shape[0], min(256, left.shape[1])
    count, columns = len(rights), rights[0].shape[1]
    return pl.pallas_call(
        functools.partial(grads_body, count),
        grid=(left.shape[1] // width,),
        in_specs=[pl.BlockSpec((tokens, width), lambda i: (0, i))]
        + [pl.BlockSpec(right.shape, lambda i: (0, 0)) for right in rights]
        + anywhere(len(earlier)),
        out_specs=pl.BlockSpec((count, width, columns), lambda i: (0, i, 0)),
        out_shape=jax.ShapeDtypeStruct((count, left.shape[1], columns), BF),
        compiler_params=pltpu.CompilerParams(vmem_limit_bytes=40 * 2**20),
        cost_estimate=cost(2 * count * tokens * left.shape[1] * columns),
        name="grads",
    )(left, *rights, *earlier)


def down_grads_body(count, *refs):
    block, out = refs[0][...], refs[-1]
    for i in range(count):
        out[i, 0] = mm_tn(refs[1 + i][...], block).astype(BF)


def down_grads(upstream, hidden, *earlier):
    ways = lax.axis_size("t")
    tokens, width = upstream.shape[0], upstream.shape[1] // ways
    count, columns = len(hidden), hidden[0].shape[1]
    return pl.pallas_call(
        functools.partial(down_grads_body, count),
        grid=(ways,),
        in_specs=[pl.BlockSpec((tokens, width), lambda i: (0, i))]
        + [pl.BlockSpec(left.shape, lambda i: (0, 0)) for left in hidden]
        + anywhere(len(earlier)),
        out_specs=pl.BlockSpec((count, 1, columns, width), lambda i: (0, i, 0, 0)),
        out_shape=jax.ShapeDtypeStruct((count, ways, columns, width), BF),
        compiler_params=pltpu.CompilerParams(vmem_limit_bytes=40 * 2**20),
        cost_estimate=cost(2 * count * tokens * upstream.shape[1] * columns),
        name="down_grads",
    )(upstream, *hidden, *earlier)


def scatter_grad(stacked):
    flat = stacked.reshape((-1,) + stacked.shape[2:])
    return lax.psum_scatter(flat, ("s", "y", "c"), scatter_dimension=0, tiled=True)


def back_body(upstream, weight, out):
    width = weight.shape[3]
    total = mm_nt(upstream[:, :width], weight[0, 0])
    for i in range(1, weight.shape[1]):
        total = total + mm_nt(upstream[:, i * width : (i + 1) * width], weight[0, i])
    out[...] = total.astype(BF)


def back_hidden(upstream, weight, s):
    tokens = upstream.shape[0]
    rows = min(256, tokens)
    return pl.pallas_call(
        back_body,
        grid=(tokens // rows,),
        in_specs=[
            pl.BlockSpec((rows, upstream.shape[1]), lambda i: (i, 0)),
            pl.BlockSpec((1,) + weight.shape[1:], lambda i: (s, 0, 0, 0)),
        ],
        out_specs=pl.BlockSpec((rows, weight.shape[2]), lambda i: (i, 0)),
        out_shape=jax.ShapeDtypeStruct((tokens, weight.shape[2]), BF),
        compiler_params=pltpu.CompilerParams(vmem_limit_bytes=40 * 2**20),
        cost_estimate=cost(2 * tokens * upstream.shape[1] * weight.shape[2]),
        name="back_hidden",
    )(upstream, weight)


def project_body(count, left, factor, *refs):
    for right, out in zip(refs[:count], refs[-count:]):
        out[...] = (mm(left[...], right[0]) * factor[...]).astype(BF)


def project(left, weights, factor):
    tokens = left.shape[0]
    rows = min(256, tokens)
    by_rows = lambda n: pl.BlockSpec((rows, n), lambda i: (i, 0))
    return pl.pallas_call(
        functools.partial(project_body, len(weights)),
        grid=(tokens // rows,),
        in_specs=[by_rows(left.shape[1]), by_rows(1)]
        + [pl.BlockSpec((1,) + w.shape[1:], lambda i, s=s: (s, 0, 0)) for w, s in weights],
        out_specs=[by_rows(w.shape[2]) for w, s in weights],
        out_shape=[jax.ShapeDtypeStruct((tokens, w.shape[2]), BF) for w, s in weights],
        compiler_params=pltpu.CompilerParams(vmem_limit_bytes=40 * 2**20),
        cost_estimate=cost(2 * tokens * left.shape[1] * sum(w.shape[2] for w, s in weights)),
        name="project",
    )(left, factor, *[w for w, s in weights])


def feed_body(scaled, factor, back, weight, hidden, dboth):
    scale = factor[...]
    gate, up = unpack(mm(scaled[...], weight[0]) * scale)
    upstream = back[...].astype(F32)
    sigmoid = 1.0 / (1.0 + jnp.exp(-gate))
    active = gate * sigmoid
    hidden[...] = (active * up).astype(BF)
    slope = upstream * up * sigmoid * (1.0 + gate * (1.0 - sigmoid))
    dgate, dup = (slope * scale).astype(BF), (upstream * active * scale).astype(BF)
    cut = dgate.shape[1] // HV * HV
    dboth[:, :cut] = dgate[:, :cut]
    dboth[:, cut : 2 * cut] = dup[:, :cut]
    dboth[:, 2 * cut :] = jnp.concatenate([dgate[:, cut:], dup[:, cut:]], axis=1)


def feed_forward(scaled, factor, back, weight, s):
    tokens, columns = back.shape
    rows = min(256, tokens)
    by_rows = lambda n: pl.BlockSpec((rows, n), lambda i: (i, 0))
    return pl.pallas_call(
        feed_body,
        grid=(tokens // rows,),
        in_specs=[
            by_rows(scaled.shape[1]),
            by_rows(1),
            by_rows(columns),
            pl.BlockSpec((1,) + weight.shape[1:], lambda i: (s, 0, 0)),
        ],
        out_specs=[by_rows(columns), by_rows(2 * columns)],
        out_shape=[jax.ShapeDtypeStruct((tokens, n), BF) for n in (columns, 2 * columns)],
        compiler_params=pltpu.CompilerParams(vmem_limit_bytes=40 * 2**20),
        cost_estimate=cost(4 * tokens * scaled.shape[1] * columns),
        name="feed_forward",
    )(scaled, factor, back, weight)


def forward_body(heads, tokens, wqk, rest, far_v, far_w, docs_c, docs_r, out, den):
    lanes = heads * HV
    for i in range(heads):
        at = i * HV
        qs, ks = 2 * lanes + i * FEAT, 2 * lanes + (heads + i) * FEAT
        fs = lanes + (heads + i) * FEAT
        for b in range(tokens // QB):
            rows = slice(b * QB, (b + 1) * QB)
            q = rest[rows, qs : qs + FEAT]
            docs_q = docs_c[REACH + b * QB : REACH + (b + 1) * QB, :]
            numer = jnp.zeros((QB, HV), F32)
            denom = jnp.zeros((QB, 1), F32)
            for kb in range(b - REACH // QB, b + 1):
                if kb >= 0:
                    keys = slice(kb * QB, (kb + 1) * QB)
                    k = rest[keys, ks : ks + FEAT]
                    v = rest[keys, lanes + at : lanes + at + HV]
                else:
                    keys = slice(REACH + kb * QB, REACH + (kb + 1) * QB)
                    k = far_v[keys, fs : fs + FEAT]
                    v = far_v[keys, at : at + HV]
                inner = mm_nt(q, k) * 0.25
                kernel = 1.0 + inner + 0.5 * inner * inner
                allowed = docs_q == docs_r[:, REACH + kb * QB : REACH + (kb + 1) * QB]
                if kb == b:
                    allowed = allowed & (
                        lax.broadcasted_iota(jnp.int32, (QB, QB), 0)
                        >= lax.broadcasted_iota(jnp.int32, (QB, QB), 1)
                    )
                kernel = jnp.where(allowed, kernel, 0.0)
                denom = denom + jnp.sum(kernel, axis=1, keepdims=True)
                numer = numer + mm(kernel.astype(BF), v)
            out[rows, at : at + HV] = (numer / denom).astype(BF)
            den[rows, i : i + 1] = denom
        for b in range(tokens // WB):
            rows = slice(b * WB, (b + 1) * WB)
            q = wqk[rows, at : at + HV]
            k, v, allowed = window_block(b, at, lanes, wqk, rest, far_w, docs_c, docs_r)
            probs = window_probs(q, k, allowed)
            out[rows, lanes + at : lanes + at + HV] = mm(probs.astype(BF), v).astype(BF)


def window_block(b, at, lanes, wqk, rest, far_w, docs_c, docs_r):
    if b:
        keys = slice((b - 1) * WB, (b + 1) * WB)
        k = wqk[keys, lanes + at : lanes + at + HV]
        v = rest[keys, at : at + HV]
    else:
        k = jnp.concatenate(
            [far_w[:, at : at + HV], wqk[:WB, lanes + at : lanes + at + HV]], axis=0
        )
        v = jnp.concatenate(
            [
                far_w[:, lanes + at : lanes + at + HV],
                rest[:WB, at : at + HV],
            ],
            axis=0,
        )
    start = REACH + b * WB
    back = (
        lax.broadcasted_iota(jnp.int32, (WB, 2 * WB), 0)
        + WB
        - lax.broadcasted_iota(jnp.int32, (WB, 2 * WB), 1)
    )
    same = docs_c[start : start + WB, :] == docs_r[:, start - WB : start + WB]
    return k, v, same & (back >= 0) & (back < WIN)


def window_probs(q, k, allowed):
    scores = jnp.where(allowed, mm_nt(q, k) * SCALE, MASKED)
    exponent = jnp.exp(scores - jnp.max(scores, axis=1, keepdims=True))
    return exponent / jnp.sum(exponent, axis=1, keepdims=True)


def backward_body(
    heads, tokens, wqk, rest, far_v, far_w, docs_c, docs_r, out, den, dout,
    *rest_refs,
):
    dwqk, drest, dfar_v, dfar_w, acc_v, acc_k, acc_wk, acc_wv = rest_refs[-8:]
    lanes = heads * HV
    lane_zero = (lax.broadcasted_iota(jnp.int32, (QB, HV), 1) == 0).astype(BF)
    dfar_v[:, lanes:] = jnp.zeros((REACH, dfar_v.shape[1] - lanes), BF)
    drest[:, 2 * lanes :] = jnp.zeros((tokens, drest.shape[1] - 2 * lanes), BF)
    for i in range(heads):
        at = i * HV
        qs, ks = 2 * lanes + i * FEAT, 2 * lanes + (heads + i) * FEAT
        fs = lanes + (heads + i) * FEAT
        acc_v[...] = jnp.zeros_like(acc_v)
        acc_k[...] = jnp.zeros_like(acc_k)
        acc_wk[...] = jnp.zeros_like(acc_wk)
        acc_wv[...] = jnp.zeros_like(acc_wv)
        for b in range(tokens // QB):
            rows = slice(b * QB, (b + 1) * QB)
            q = rest[rows, qs : qs + FEAT]
            docs_q = docs_r[:, REACH + b * QB : REACH + (b + 1) * QB]
            dlin = dout[rows, at : at + HV].astype(F32)
            inverse = 1.0 / den[rows, i : i + 1]
            mean = jnp.sum(dlin * out[rows, at : at + HV].astype(F32), axis=1, keepdims=True)
            dnumer = (dlin * inverse).astype(BF)
            ddenom = (-mean * inverse).astype(BF)
            extended = jnp.concatenate([dnumer, ddenom * lane_zero], axis=1)
            dq = jnp.zeros((QB, FEAT), F32)
            for kb in range(b - REACH // QB, b + 1):
                place = slice(REACH + kb * QB, REACH + (kb + 1) * QB)
                if kb >= 0:
                    keys = slice(kb * QB, (kb + 1) * QB)
                    k = rest[keys, ks : ks + FEAT]
                    v = rest[keys, lanes + at : lanes + at + HV]
                else:
                    k = far_v[place, fs : fs + FEAT]
                    v = far_v[place, at : at + HV]
                inner = mm_nt(k, q) * 0.25
                weight = mm_nt(jnp.concatenate([v, lane_zero], axis=1), extended)
                allowed = docs_c[place, :] == docs_q
                if kb == b:
                    allowed = allowed & (
                        lax.broadcasted_iota(jnp.int32, (QB, QB), 0)
                        <= lax.broadcasted_iota(jnp.int32, (QB, QB), 1)
                    )
                kernel = jnp.where(allowed, 1.0 + inner + 0.5 * inner * inner, 0.0).astype(BF)
                slope = jnp.where(allowed, weight * (0.25 + 0.25 * inner), 0.0).astype(BF)
                acc_v[place, :] += mm(kernel, dnumer)
                acc_k[place, :] += mm(slope, q)
                dq = dq + mm_tn(slope, k)
            drest[rows, qs : qs + FEAT] = dq.astype(BF)
        dfar_v[:, at : at + HV] = acc_v[:REACH, :].astype(BF)
        dfar_v[:, fs : fs + FEAT] = acc_k[:REACH, :].astype(BF)
        drest[:, lanes + at : lanes + at + HV] = acc_v[REACH:, :].astype(BF)
        drest[:, ks : ks + FEAT] = acc_k[REACH:, :].astype(BF)
        for b in range(tokens // WB):
            rows = slice(b * WB, (b + 1) * WB)
            q = wqk[rows, at : at + HV]
            k, v, allowed = window_block(b, at, lanes, wqk, rest, far_w, docs_c, docs_r)
            probs = window_probs(q, k, allowed)
            upstream = dout[rows, lanes + at : lanes + at + HV]
            dprobs = mm_nt(upstream, v)
            dscores = probs * (dprobs - jnp.sum(probs * dprobs, axis=1, keepdims=True))
            dscores = dscores.astype(BF)
            dwqk[rows, at : at + HV] = (mm(dscores, k) * SCALE).astype(BF)
            span = slice(b * WB, (b + 2) * WB)
            acc_wk[span, :] += mm_tn(dscores, q)
            acc_wv[span, :] += mm_tn(probs.astype(BF), upstream)
        dfar_w[:, at : at + HV] = (acc_wk[:WB, :] * SCALE).astype(BF)
        dfar_w[:, lanes + at : lanes + at + HV] = acc_wv[:WB, :].astype(BF)
        dwqk[:, lanes + at : lanes + at + HV] = (acc_wk[WB:, :] * SCALE).astype(BF)
        drest[:, at : at + HV] = acc_wv[WB:, :].astype(BF)


VMEM = pltpu.CompilerParams(vmem_limit_bytes=28 * 2**20)


def attention_forward(heads, wqk, rest, far_v, far_w, docs_c, docs_r):
    tokens = wqk.shape[0]
    outs = (
        jax.ShapeDtypeStruct((tokens, 2 * heads * HV), BF),
        jax.ShapeDtypeStruct((tokens, heads), F32),
    )
    return pl.pallas_call(
        functools.partial(forward_body, heads, tokens),
        out_shape=outs,
        compiler_params=VMEM,
        cost_estimate=cost(6e9),
        name="attention_forward",
    )(wqk, rest, far_v, far_w, docs_c, docs_r)


def attention_backward(heads, wqk, rest, far_v, far_w, docs_c, docs_r, out, den, dout, *earlier):
    tokens = wqk.shape[0]
    ins = (wqk, rest, far_v, far_w, docs_c, docs_r, out, den, dout)
    return pl.pallas_call(
        functools.partial(backward_body, heads, tokens),
        in_specs=[pl.BlockSpec(memory_space=pltpu.VMEM)] * len(ins) + anywhere(len(earlier)),
        out_shape=tuple(jax.ShapeDtypeStruct(a.shape, BF) for a in (wqk, rest, far_v, far_w)),
        scratch_shapes=[
            pltpu.VMEM((REACH + tokens, HV), F32),
            pltpu.VMEM((REACH + tokens, FEAT), F32),
            pltpu.VMEM((WB + tokens, HV), F32),
            pltpu.VMEM((WB + tokens, HV), F32),
        ],
        compiler_params=VMEM,
        cost_estimate=cost(17e9),
        name="attention_backward",
    )(*ins, *earlier)


def feature_tables():
    pick_a = np.zeros((F1, F1 * F1), np.float32)
    pick_b = np.zeros((F1, F1 * F1), np.float32)
    scale = np.ones((F1 * F1,), np.float32)
    for r in range(F1):
        for j in range(F1):
            f = r * F1 + j
            pick_a[r, f] = 1.0
            if r < FEAT:
                scale[f] = HALF_ROOT
                if j < FEAT:
                    pick_b[j, f] = 1.0
            else:
                pick_b[FEAT if j == 0 else j - 1, f] = 1.0
    return pick_a, pick_b, scale


def row_states(heads, keys, values, docs):
    keys, values = keys[:, -REACH:], values[:, -REACH:]
    keys = jnp.swapaxes(keys.reshape(2, REACH, heads, FEAT), 1, 2).reshape(-1, REACH, FEAT)
    values = jnp.swapaxes(values.reshape(2, REACH, heads, HV), 1, 2).reshape(-1, REACH, HV)
    ones = jnp.ones(keys.shape[:2] + (1,), BF)
    extended = jnp.concatenate([keys * BF(0.5), ones], axis=2)
    pick_a, pick_b, scale = feature_tables()
    left = jnp.einsum("bsf,fg->bsg", extended, jnp.asarray(pick_a, BF), preferred_element_type=F32)
    right = jnp.einsum("bsf,fg->bsg", extended, jnp.asarray(pick_b, BF), preferred_element_type=F32)
    in_last = (docs[-REACH:] == docs[-1]).astype(F32)
    features = left * right * scale * in_last[None, :, None]
    return jnp.einsum("bsg,bsv->bgv", features.astype(BF), values, preferred_element_type=F32)


def owned_states(heads, states, owner):
    ways = lax.axis_size("t")
    mine_t, side = lax.axis_index("t"), lax.axis_index("s")
    states = lax.all_gather(states.astype(BF), ("c", "s", "t"), axis=0, tiled=False)
    states = lax.dynamic_slice_in_dim(states, (2 + lax.axis_index("c")) * ways, ways, 0)
    states = states.reshape(GROUPS, F1, HV)
    slots = GROUPS // ways
    groups = jnp.arange(GROUPS, dtype=jnp.int32)
    mine = owner == 2 * mine_t + side
    ordinal = jnp.sum((mine[None, :] & (groups[None, :] < groups[:, None])).astype(jnp.int32), axis=1)
    wanted = jnp.arange(slots, dtype=jnp.int32)
    picked = (mine[None, :] & (ordinal[None, :] == wanted[:, None])).astype(BF)
    return jnp.einsum("kg,gfv->kfv", picked, states, preferred_element_type=F32)[None]


def momentum_update(weights, moment, average, gradient, factor, token_total):
    step_rate = factor / math.sqrt(token_total)
    moment_new = MOMENTUM * moment + gradient
    weights_new = weights - step_rate * (gradient + MOMENTUM * moment_new)
    average_new = AVERAGE_OLD * average + AVERAGE_NEW * weights_new
    return (gradient, weights_new, moment_new, average_new, weights_new.astype(BF))


def norm_back(values, factor, gains, upstream):
    gain_grad = jnp.sum(upstream * values, axis=0)
    inner = total_t(jnp.sum(upstream * gains * values, axis=1))
    scale = factor * factor * inner[:, None] / D
    return gains * upstream - values * scale, gain_grad


def local(
    layer_in, out_grad, doc_ids, group_owner,
    norm_gains, norm_gains_moment, norm_gains_average,
    feature_proj, feature_proj_moment, feature_proj_average,
    head_proj, head_proj_moment, head_proj_average,
    mixer_out, mixer_out_moment, mixer_out_average,
    gate_up, gate_up_moment, gate_up_average,
    down_proj, down_proj_moment, down_proj_average,
):
    data_ways = lax.axis_size("y") * 2
    core, side = lax.axis_index("c"), lax.axis_index("s")
    width = layer_in.shape[1]
    tokens = layer_in.shape[0] // 2
    heads = head_proj.shape[2] // HV
    rows = head_proj.shape[0]
    lanes = heads * HV
    token_total = layer_in.shape[0] * data_ways

    x_low = enter(layer_in)
    x = x_low.astype(F32)
    other_gains = lax.ppermute(norm_gains, "s", [(0, 1), (1, 0)])
    gains = jnp.where(
        side == 0,
        jnp.concatenate([norm_gains, other_gains], axis=1),
        jnp.concatenate([other_gains, norm_gains], axis=1),
    )
    docs = lax.ppermute(doc_ids, ("c", "s"), SWAP)
    docs = jnp.concatenate([jnp.full((1, REACH), -1, jnp.int32), docs], axis=1)
    docs_r = lax.dynamic_slice_in_dim(docs, core * tokens, REACH + tokens, 1)
    docs_c = jnp.reshape(docs_r, (REACH + tokens, 1))

    scaled_mine = (x * gains[0]).astype(BF)
    wqk_shard = head_proj[:, :2].reshape(rows, -1)
    extra = -(2 * heads * FEAT) % HV
    rest_shard = jnp.concatenate(
        [head_proj[:, 2:].reshape(rows, -1), feature_proj.reshape(rows, -1), jnp.zeros((rows, extra), F32)], axis=1
    )
    parts = send_t(scaled_mine)
    wqk_full = rows_of(gather_weight(wqk_shard, x_low))
    rest_full = rows_of(gather_weight(rest_shard, x_low))
    begun = parts[3:5]
    mixer_full = rows_of(gather_weight(jnp.transpose(mixer_out, (2, 0, 1)).reshape(rows, -1), *begun))
    both_full = rows_of(gather_weight(pack(gate_up), *begun))
    down_full = gather_weight(down_proj, *begun)
    factor_one = lax.rsqrt(total_t(jnp.sum(x * x, axis=1)) / D + EPSILON)[:, None]
    scaled_one = join_t(parts)
    dy_mine = enter(out_grad, *begun)
    dy = lax.all_gather(dy_mine, "t", axis=1, tiled=True)
    wqk, rest = [], []
    for s in range(2):
        one, two = project(scaled_one, [(wqk_full, s), (rest_full, s)], factor_one)
        wqk.append(one)
        rest.append(two)

    ahead, behind = [(0, 1)], [(1, 0)]
    far_v = [lax.ppermute(p[-REACH:, lanes:], "c", ahead) for p in rest]
    far_w = [
        lax.ppermute(jnp.concatenate([a[-WB:, lanes:], b[-WB:, :lanes]], axis=1), "c", ahead)
        for a, b in zip(wqk, rest)
    ]
    attended, denom = [], []
    for s in range(2):
        one, two = attention_forward(heads, wqk[s], rest[s], far_v[s], far_w[s], docs_c, docs_r)
        attended.append(one)
        denom.append(two)

    mixed = add_up(spread_t(attended, both_s(mixer_full))[0])
    middle = x + mixed
    factor_two = lax.rsqrt(total_t(jnp.sum(middle * middle, axis=1)) / D + EPSILON)[:, None]
    scaled_mine = (middle * gains[1]).astype(BF)
    parts = send_t(scaled_mine)
    dhidden = [back_hidden(dy, down_full, s) for s in range(2)]
    last = jnp.stack([p[-REACH:, lanes:] for p in rest])
    states = row_states(heads, last[:, :, lanes + heads * FEAT : lanes + 2 * heads * FEAT], last[:, :, :lanes], docs_r[0])
    row_state = owned_states(heads, states, group_owner)
    scaled_two = join_t(parts, *dhidden)

    hidden, dboth = [], []
    for s in range(2):
        one, two = feed_forward(scaled_two, factor_two, dhidden[s], both_full, s)
        hidden.append(one)
        dboth.append(two)
    parts, second = spread_t(dboth, both_s(both_full), row_state)
    for_down = down_grads(dy, hidden, *second[:2])
    upstream_two = add_up([hold(parts[0], for_down)] + parts[1:])
    back_two, gain_two = norm_back(middle, factor_two, gains[1], upstream_two)
    dmixed_mine = (dy_mine.astype(F32) + back_two).astype(BF)
    parts = send_t(dmixed_mine)
    for_both = grads(scaled_two, dboth, *parts[1:3])
    branch_parts, second = spread_t(hidden, both_s(down_full), for_both, *parts[3:5])
    dmixed = join_t(parts, for_both)
    down_sum, both_sum = scatter_grad(for_down), scatter_grad(for_both)

    branch = add_up(branch_parts)
    out_y = layer_in + leave((mixed + branch).astype(BF)).astype(F32)
    dattended = project(dmixed, both_s(mixer_full), jnp.ones((tokens, 1), F32))
    mixer_sum = scatter_grad(hold(grads(dmixed, attended, *dattended), both_sum))
    dwqk, drest = [], []
    for s in range(2):
        one, two, three, four = attention_backward(
            heads, wqk[s], rest[s], far_v[s], far_w[s], docs_c, docs_r, attended[s], denom[s], dattended[s], *second[2 * s : 2 * s + 2]
        )
        far_three = lax.ppermute(three, "c", behind).astype(F32)
        far_four = lax.ppermute(four, "c", behind).astype(F32)
        one = one.astype(F32) + jnp.pad(far_four[:, :lanes], ((tokens - WB, 0), (lanes, 0)))
        two = (
            two.astype(F32)
            + jnp.pad(far_three, ((tokens - REACH, 0), (lanes, 0)))
            + jnp.pad(far_four[:, lanes:], ((tokens - WB, 0), (0, rest[s].shape[1] - lanes)))
        )
        dwqk.append((one * factor_one).astype(BF))
        drest.append((two * factor_one).astype(BF))
    parts, second = spread_t(dwqk + drest, both_s(wqk_full) + both_s(rest_full), down_sum, both_sum, branch)
    rest_sum = scatter_grad(grads(scaled_one, drest, *second[:2]))
    wqk_sum = scatter_grad(grads(scaled_one, dwqk, *second[:2]))
    upstream_one = add_up([hold(parts[0], mixer_sum)] + parts[1:])
    back_one, gain_one = norm_back(x, factor_one, gains[0], upstream_one)
    grad_x = out_grad + leave((back_one + back_two).astype(BF)).astype(F32)
    wqk_sum, rest_sum, mixer_sum, both_sum = [a.astype(F32) for a in (wqk_sum, rest_sum, mixer_sum, both_sum)]
    down_sum = down_sum[0].astype(F32)
    head_sum = jnp.concatenate([wqk_sum, rest_sum[:, : 2 * lanes]], axis=1)
    feature_sum = rest_sum[:, 2 * lanes : 2 * lanes + 2 * heads * FEAT]

    both = jnp.stack([gain_one, gain_two], axis=0)
    both = both + peer(both, "c", 1)
    step = 1
    while step < data_ways // 2:
        both = both + peer(both, "y", step)
        step *= 2
    low, high = both[:, :width], both[:, width:]
    gains_sum = jnp.where(side == 0, low, high) + peer(jnp.where(side == 0, high, low), "s", 1)

    mixer_sum = jnp.transpose(mixer_sum.reshape(rows, 2, lanes), (1, 2, 0))
    triples = (
        (norm_gains, norm_gains_moment, norm_gains_average, gains_sum),
        (feature_proj, feature_proj_moment, feature_proj_average, feature_sum.reshape(feature_proj.shape)),
        (head_proj, head_proj_moment, head_proj_average, head_sum.reshape(head_proj.shape)),
        (mixer_out, mixer_out_moment, mixer_out_average, mixer_sum),
        (gate_up, gate_up_moment, gate_up_average, jnp.stack(unpack(both_sum), axis=1)),
        (down_proj, down_proj_moment, down_proj_average, down_sum),
    )
    results = [out_y, grad_x, row_state]
    for index, triple in enumerate(triples):
        results.extend(momentum_update(*triple, RATE_FACTORS[index], token_total))
    return tuple(results)


def solution(mesh):
    data_ways, model_ways = mesh.shape["dp"], mesh.shape["mp"]
    grid = Mesh(mesh.devices.reshape(data_ways // 2, 2, model_ways // 2, 2), ("y", "c", "t", "s"))
    dp, mp = ("y", "c"), ("t", "s")
    gains = (P(None, mp),)
    rows_cols = (P(dp, None, mp),)
    mixer = (P(None, mp, dp),)
    down = (P(mp, dp),)
    tokens = (P(dp, mp),)
    return jax.shard_map(
        local,
        mesh=grid,
        in_specs=tokens * 2
        + (P(dp, None), P())
        + gains * 3
        + rows_cols * 6
        + mixer * 3
        + rows_cols * 3
        + down * 3,
        out_specs=tokens * 2
        + (P(dp, mp, None, None),)
        + gains * 5
        + rows_cols * 10
        + mixer * 5
        + rows_cols * 5
        + down * 5,
        check_vma=False,
    )
```

```python
import functools
import math

import jax
import jax.numpy as jnp
import numpy as np
from jax import lax
from jax.experimental import pallas as pl
from jax.experimental.pallas import tpu as pltpu
from jax.sharding import Mesh, PartitionSpec as P

D = 2048
HEADS = 16
FEAT = 16
HV = 128
WIN = 64
F1 = 17
GROUPS = 272
REACH = 512
QB = 256
WB = 128

EPSILON = 1e-05
MOMENTUM = 0.9
AVERAGE_OLD = 0.99 * 0.01 / (1.0 - 0.99 * 0.99)
AVERAGE_NEW = 0.01 / (1.0 - 0.99 * 0.99)
RATE_FACTORS = (0.03, 0.01, 0.01, 0.28, 0.029, 0.01)
HALF_ROOT = 0.7071067811865476
MASKED = -1e30
SCALE = HV**-0.5
BF = jnp.bfloat16
F32 = jnp.float32


def cost(matmul_flops):
    return pl.CostEstimate(flops=int(0.05 * matmul_flops), bytes_accessed=1, transcendentals=0)


CHEAP = cost(0)
NT = (((1,), (1,)), ((), ()))
TN = (((0,), (0,)), ((), ()))


def mm(left, right):
    return jnp.dot(left, right, preferred_element_type=F32)


def mm_nt(left, right):
    return lax.dot_general(left, right, NT, preferred_element_type=F32)


def mm_tn(left, right):
    return lax.dot_general(left, right, TN, preferred_element_type=F32)


def peer(values, axis, offset):
    ways = lax.axis_size(axis)
    return lax.ppermute(values, axis, [(i, i ^ offset) for i in range(ways)])


def shift(values, step, first):
    ways = lax.axis_size("t")
    places = range(first, ways - 1) if step > 0 else range(1, ways - first)
    return lax.ppermute(values, "t", [(i, i + step) for i in places])


SWAP = [(2 * a + b, 2 * b + a) for a in range(2) for b in range(2)]
TURN = [(2 * a + b, 2 * (1 - b) + a) for a in range(2) for b in range(2)]
BACK = [(2 * (1 - b) + a, 2 * a + b) for a in range(2) for b in range(2)]


def told(flag, *earlier):
    flag = flag.astype(jnp.int32).reshape(1, 1)
    return (hold(flag, *earlier) if earlier else flag)[0, 0] == 1


def enter(values, *earlier):
    half = values.shape[0] // 2
    near = told(lax.axis_index("s") == 0, *earlier)
    first = jnp.where(near, values[:half], values[half:]).astype(BF)
    second = jnp.where(near, values[half:], values[:half]).astype(BF)
    same = lax.ppermute(first, ("c", "s"), SWAP)
    other = lax.ppermute(second, ("c", "s"), TURN)
    low = lax.axis_index("c") == 0
    return jnp.concatenate([jnp.where(low, same, other), jnp.where(low, other, same)], axis=1)


def leave(values):
    width = values.shape[1] // 2
    low = lax.axis_index("c") == 0
    same = jnp.where(low, values[:, :width], values[:, width:])
    other = jnp.where(low, values[:, width:], values[:, :width])
    same = lax.ppermute(same, ("c", "s"), SWAP)
    other = lax.ppermute(other, ("c", "s"), BACK)
    near = lax.axis_index("s") == 0
    return jnp.concatenate([jnp.where(near, same, other), jnp.where(near, other, same)], axis=0)


def line():
    return lax.axis_size("t") == 4


def send_t(piece):
    ways = lax.axis_size("t")
    if not line():
        return [piece] + [peer(piece, "t", offset) for offset in range(1, ways)]
    parts = [piece]
    up = down = piece
    for step in range(ways - 1):
        up, down = shift(up, 1, step), shift(down, -1, step)
        parts += [up, down]
    return parts


def where_from(mine, place):
    if not line():
        return mine ^ place
    return 0 if mine == place else 2 * abs(mine - place) - (1 if place < mine else 0)


def anywhere(count):
    return [pl.BlockSpec(memory_space=pl.ANY)] * count


def hold(values, *earlier):
    def body(*refs):
        pass

    return pl.pallas_call(
        body,
        out_shape=jax.ShapeDtypeStruct(values.shape, values.dtype),
        in_specs=anywhere(1 + len(earlier)),
        out_specs=pl.BlockSpec(memory_space=pl.ANY),
        input_output_aliases={0: 0},
        cost_estimate=CHEAP,
        name="hold",
    )(values, *earlier)


def join_body(ways, mine, *refs):
    parts, out = refs, refs[-1]
    width = parts[0].shape[1]
    for d in range(ways):

        @pl.when(mine[0] == d)
        def _():
            for place in range(ways):
                out[:, place * width : (place + 1) * width] = parts[where_from(d, place)][...]


def join_t(parts, *earlier):
    ways = lax.axis_size("t")
    tokens, width = parts[0].shape
    rows = min(256, tokens)
    return pl.pallas_call(
        functools.partial(join_body, ways),
        grid_spec=pltpu.PrefetchScalarGridSpec(
            num_scalar_prefetch=1,
            grid=(tokens // rows,),
            in_specs=[pl.BlockSpec((rows, width), lambda i, mine: (i, 0))] * len(parts)
            + anywhere(len(earlier)),
            out_specs=pl.BlockSpec((rows, ways * width), lambda i, mine: (i, 0)),
        ),
        out_shape=jax.ShapeDtypeStruct((tokens, ways * width), parts[0].dtype),
        cost_estimate=cost(5e9),
        name="join",
    )(lax.axis_index("t").astype(jnp.int32).reshape(1), *parts, *earlier)


def terms_body(count, pieces, dests, *refs):
    lefts, rights, outs = refs[:count], refs[count : 2 * count], refs[-pieces:]
    total = None
    for left, right in zip(lefts, rights):
        if len(right.shape) == 4:
            product = mm(left[...], right[0, 0])
        else:
            product = mm_nt(left[...], right[0])
        total = product if total is None else total + product
    for i in range(pieces):

        @pl.when(pl.program_id(0) == i)
        def _():
            outs[i][...] = total.astype(outs[i].dtype)


def terms_t(lefts, rights, dests, dtypes, *earlier):
    tokens = lefts[0].shape[0]
    count, pieces = len(lefts), len(dtypes)
    width = D // lax.axis_size("t")

    def right_spec(weight, s):
        if len(weight.shape) == 4:
            return pl.BlockSpec((1, 1) + weight.shape[2:], lambda i, dests: (s, dests[i], 0, 0))
        return pl.BlockSpec((1, width, weight.shape[2]), lambda i, dests: (s, dests[i], 0))

    return pl.pallas_call(
        functools.partial(terms_body, count, pieces),
        grid_spec=pltpu.PrefetchScalarGridSpec(
            num_scalar_prefetch=1,
            grid=(pieces,),
            in_specs=[pl.BlockSpec(a.shape, lambda i, dests: (0, 0)) for a in lefts]
            + [right_spec(*right) for right in rights]
            + anywhere(len(earlier)),
            out_specs=[pl.BlockSpec((tokens, width), lambda i, dests: (0, 0))] * pieces,
        ),
        out_shape=[jax.ShapeDtypeStruct((tokens, width), dtype) for dtype in dtypes],
        compiler_params=pltpu.CompilerParams(vmem_limit_bytes=48 * 2**20),
        cost_estimate=cost(2 * pieces * tokens * width * sum(a.shape[1] for a in lefts)),
        name="terms",
    )(dests, *lefts, *[weight for weight, s in rights], *earlier)


def pieces_t(lefts, rights, *earlier):
    return terms_t(lefts, rights, line_order(), [BF, BF, BF, F32], *earlier)


def hop(values, step, count):
    places = range(count) if step > 0 else range(3, 3 - count, -1)
    return lax.ppermute(values, "t", [(i, i + step) for i in places])


def both_s(weight):
    return [(weight, 0), (weight, 1)]


def spread_t(lefts, rights, *earlier):
    ways, mine = lax.axis_size("t"), lax.axis_index("t")
    if not line():
        dests = jnp.stack([mine ^ offset for offset in range(ways)]).astype(jnp.int32)
        parts = terms_t(lefts, rights, dests, [F32] + [BF] * (ways - 1), *earlier)
        return [parts[0]] + [peer(part, "t", offset) for offset, part in enumerate(parts) if offset], parts
    dests = line_order()
    [first] = terms_t(lefts, rights, dests[:1], [BF], *earlier)
    return along_line(first, *terms_t(lefts, rights, dests[1:], [BF, BF, F32], first))


def line_order():
    order = jnp.asarray(np.array([[3, 2, 1, 0], [3, 2, 0, 1], [0, 1, 3, 2], [0, 1, 2, 3]], np.int32))
    return lax.dynamic_index_in_dim(order, lax.axis_index("t"), 0, False)


def along_line(first, second, third, own):
    mine = lax.axis_index("t")
    up, down = hop(first, 1, 1), hop(first, -1, 1)
    wide = lambda a: a.astype(F32)
    up2 = (jnp.where(mine == 0, wide(second), wide(first)) + wide(up)).astype(BF)
    down2 = (jnp.where(mine == 3, wide(second), wide(first)) + wide(down)).astype(BF)
    up, down = hop(up2, 1, 2), hop(down2, -1, 2)
    up3 = (jnp.where(mine == 1, wide(second), wide(third)) + wide(up)).astype(BF)
    down3 = (jnp.where(mine == 2, wide(second), wide(third)) + wide(down)).astype(BF)
    return [own, hop(up3, 1, 3), hop(down3, -1, 3)], [up2, down2, up3, down3]


def add_up(parts):
    total = parts[0].astype(F32)
    for part in parts[1:]:
        total = total + part.astype(F32)
    return total


def total_t(values):
    total = values
    for offset in range(1, lax.axis_size("t")):
        total = total + peer(values, "t", offset)
    return total


def rounded(shard, *earlier):
    flag = told(lax.axis_index("s") >= 0, *earlier)
    return jnp.where(flag, shard, 0.0).astype(BF)


def gather_weight(shard):
    full = lax.all_gather(shard.astype(BF), ("s", "y", "c"), axis=0, tiled=False)
    return full.reshape((2, -1) + shard.shape)


def rows_of(full):
    return full.reshape(2, -1, full.shape[3])


def pack_body(pair, *refs):
    out = refs[-1]
    cut = pair.shape[2] // HV * HV
    gate, up = pair[:, 0, :].astype(BF), pair[:, 1, :].astype(BF)
    out[:, :cut] = gate[:, :cut]
    out[:, cut : 2 * cut] = up[:, :cut]
    out[:, 2 * cut :] = jnp.concatenate([gate[:, cut:], up[:, cut:]], axis=1)


def packed_rounded(pair, *earlier):
    rows, ways, columns = pair.shape
    step = min(128, rows)
    return pl.pallas_call(
        pack_body,
        grid=(rows // step,),
        in_specs=[pl.BlockSpec((step, ways, columns), lambda i: (i, 0, 0))] + anywhere(len(earlier)),
        out_specs=pl.BlockSpec((step, ways * columns), lambda i: (i, 0)),
        out_shape=jax.ShapeDtypeStruct((rows, ways * columns), BF),
        compiler_params=pltpu.CompilerParams(vmem_limit_bytes=40 * 2**20),
        cost_estimate=CHEAP,
        name="pack",
    )(pair, *earlier)


def unpack(packed):
    columns = packed.shape[1] // 2
    cut = columns // HV * HV
    left = 2 * cut
    more = columns - cut
    gate = jnp.concatenate([packed[:, :cut], packed[:, left : left + more]], axis=1)
    return gate, jnp.concatenate([packed[:, cut:left], packed[:, left + more :]], axis=1)


def grads_body(count, *refs):
    turned, out = refs[0][...].T, refs[-1]
    for i in range(count):
        out[i] = mm(turned, refs[1 + i][...]).astype(BF)


def grads(left, rights, *earlier):
    tokens, width = left.shape[0], min(256, left.shape[1])
    count, columns = len(rights), rights[0].shape[1]
    return pl.pallas_call(
        functools.partial(grads_body, count),
        grid=(left.shape[1] // width,),
        in_specs=[pl.BlockSpec((tokens, width), lambda i: (0, i))]
        + [pl.BlockSpec(right.shape, lambda i: (0, 0)) for right in rights]
        + anywhere(len(earlier)),
        out_specs=pl.BlockSpec((count, width, columns), lambda i: (0, i, 0)),
        out_shape=jax.ShapeDtypeStruct((count, left.shape[1], columns), BF),
        compiler_params=pltpu.CompilerParams(vmem_limit_bytes=40 * 2**20),
        cost_estimate=cost(2 * count * tokens * left.shape[1] * columns),
        name="grads",
    )(left, *rights, *earlier)


def down_grads_body(count, *refs):
    block, out = refs[0][...], refs[-1]
    for i in range(count):
        out[i, 0] = mm_tn(refs[1 + i][...], block).astype(BF)


def down_grads(upstream, hidden, *earlier):
    ways = lax.axis_size("t")
    tokens, width = upstream.shape[0], upstream.shape[1] // ways
    count, columns = len(hidden), hidden[0].shape[1]
    return pl.pallas_call(
        functools.partial(down_grads_body, count),
        grid=(ways,),
        in_specs=[pl.BlockSpec((tokens, width), lambda i: (0, i))]
        + [pl.BlockSpec(left.shape, lambda i: (0, 0)) for left in hidden]
        + anywhere(len(earlier)),
        out_specs=pl.BlockSpec((count, 1, columns, width), lambda i: (0, i, 0, 0)),
        out_shape=jax.ShapeDtypeStruct((count, ways, columns, width), BF),
        compiler_params=pltpu.CompilerParams(vmem_limit_bytes=40 * 2**20),
        cost_estimate=cost(2 * count * tokens * upstream.shape[1] * columns),
        name="down_grads",
    )(upstream, *hidden, *earlier)


def scatter_grad(stacked):
    flat = stacked.reshape((-1,) + stacked.shape[2:])
    return lax.psum_scatter(flat, ("s", "y", "c"), scatter_dimension=0, tiled=True)


def back_body(upstream, weight, out):
    width = weight.shape[3]
    total = mm_nt(upstream[:, :width], weight[0, 0])
    for i in range(1, weight.shape[1]):
        total = total + mm_nt(upstream[:, i * width : (i + 1) * width], weight[0, i])
    out[...] = total.astype(BF)


def back_hidden(upstream, weight, s):
    tokens = upstream.shape[0]
    rows = min(256, tokens)
    return pl.pallas_call(
        back_body,
        grid=(tokens // rows,),
        in_specs=[
            pl.BlockSpec((rows, upstream.shape[1]), lambda i: (i, 0)),
            pl.BlockSpec((1,) + weight.shape[1:], lambda i: (s, 0, 0, 0)),
        ],
        out_specs=pl.BlockSpec((rows, weight.shape[2]), lambda i: (i, 0)),
        out_shape=jax.ShapeDtypeStruct((tokens, weight.shape[2]), BF),
        compiler_params=pltpu.CompilerParams(vmem_limit_bytes=40 * 2**20),
        cost_estimate=cost(2 * tokens * upstream.shape[1] * weight.shape[2]),
        name="back_hidden",
    )(upstream, weight)


def project_body(count, left, factor, *refs):
    for right, out in zip(refs[:count], refs[-count:]):
        out[...] = (mm(left[...], right[0]) * factor[...]).astype(BF)


def project(left, weights, factor, *earlier):
    tokens = left.shape[0]
    rows = min(256, tokens)
    by_rows = lambda n: pl.BlockSpec((rows, n), lambda i: (i, 0))
    return pl.pallas_call(
        functools.partial(project_body, len(weights)),
        grid=(tokens // rows,),
        in_specs=[by_rows(left.shape[1]), by_rows(1)]
        + [pl.BlockSpec((1,) + w.shape[1:], lambda i, s=s: (s, 0, 0)) for w, s in weights]
        + anywhere(len(earlier)),
        out_specs=[by_rows(w.shape[2]) for w, s in weights],
        out_shape=[jax.ShapeDtypeStruct((tokens, w.shape[2]), BF) for w, s in weights],
        compiler_params=pltpu.CompilerParams(vmem_limit_bytes=40 * 2**20),
        cost_estimate=cost(2 * tokens * left.shape[1] * sum(w.shape[2] for w, s in weights)),
        name="project",
    )(left, factor, *[w for w, s in weights], *earlier)


def feed_body(scaled, factor, back, weight, hidden, dboth):
    scale = factor[...]
    gate, up = unpack(mm(scaled[...], weight[0]) * scale)
    upstream = back[...].astype(F32)
    sigmoid = 1.0 / (1.0 + jnp.exp(-gate))
    active = gate * sigmoid
    hidden[...] = (active * up).astype(BF)
    slope = upstream * up * sigmoid * (1.0 + gate * (1.0 - sigmoid))
    dgate, dup = (slope * scale).astype(BF), (upstream * active * scale).astype(BF)
    cut = dgate.shape[1] // HV * HV
    dboth[:, :cut] = dgate[:, :cut]
    dboth[:, cut : 2 * cut] = dup[:, :cut]
    dboth[:, 2 * cut :] = jnp.concatenate([dgate[:, cut:], dup[:, cut:]], axis=1)


def feed_forward(scaled, factor, back, weight, s):
    tokens, columns = back.shape
    rows = min(256, tokens)
    by_rows = lambda n: pl.BlockSpec((rows, n), lambda i: (i, 0))
    return pl.pallas_call(
        feed_body,
        grid=(tokens // rows,),
        in_specs=[
            by_rows(scaled.shape[1]),
            by_rows(1),
            by_rows(columns),
            pl.BlockSpec((1,) + weight.shape[1:], lambda i: (s, 0, 0)),
        ],
        out_specs=[by_rows(columns), by_rows(2 * columns)],
        out_shape=[jax.ShapeDtypeStruct((tokens, n), BF) for n in (columns, 2 * columns)],
        compiler_params=pltpu.CompilerParams(vmem_limit_bytes=40 * 2**20),
        cost_estimate=cost(4 * tokens * scaled.shape[1] * columns),
        name="feed_forward",
    )(scaled, factor, back, weight)


def forward_body(heads, tokens, wqk, rest, far_v, far_w, docs_c, docs_r, *rest_refs):
    out, den = rest_refs[-2:]
    lanes = heads * HV
    for i in range(heads):
        at = i * HV
        qs, ks = 2 * lanes + i * FEAT, 2 * lanes + (heads + i) * FEAT
        fs = lanes + (heads + i) * FEAT
        for b in range(tokens // QB):
            rows = slice(b * QB, (b + 1) * QB)
            q = rest[rows, qs : qs + FEAT]
            docs_q = docs_c[REACH + b * QB : REACH + (b + 1) * QB, :]
            numer = jnp.zeros((QB, HV), F32)
            denom = jnp.zeros((QB, 1), F32)
            for kb in range(b - REACH // QB, b + 1):
                if kb >= 0:
                    keys = slice(kb * QB, (kb + 1) * QB)
                    k = rest[keys, ks : ks + FEAT]
                    v = rest[keys, lanes + at : lanes + at + HV]
                else:
                    keys = slice(REACH + kb * QB, REACH + (kb + 1) * QB)
                    k = far_v[keys, fs : fs + FEAT]
                    v = far_v[keys, at : at + HV]
                inner = mm_nt(q, k) * 0.25
                kernel = 1.0 + inner + 0.5 * inner * inner
                allowed = docs_q == docs_r[:, REACH + kb * QB : REACH + (kb + 1) * QB]
                if kb == b:
                    allowed = allowed & (
                        lax.broadcasted_iota(jnp.int32, (QB, QB), 0)
                        >= lax.broadcasted_iota(jnp.int32, (QB, QB), 1)
                    )
                kernel = jnp.where(allowed, kernel, 0.0)
                denom = denom + jnp.sum(kernel, axis=1, keepdims=True)
                numer = numer + mm(kernel.astype(BF), v)
            out[rows, at : at + HV] = (numer / denom).astype(BF)
            den[rows, i : i + 1] = denom
        for b in range(tokens // WB):
            rows = slice(b * WB, (b + 1) * WB)
            q = wqk[rows, at : at + HV]
            k, v, allowed = window_block(b, at, lanes, wqk, rest, far_w, docs_c, docs_r)
            probs = window_probs(q, k, allowed)
            out[rows, lanes + at : lanes + at + HV] = mm(probs.astype(BF), v).astype(BF)


def window_block(b, at, lanes, wqk, rest, far_w, docs_c, docs_r):
    if b:
        keys = slice((b - 1) * WB, (b + 1) * WB)
        k = wqk[keys, lanes + at : lanes + at + HV]
        v = rest[keys, at : at + HV]
    else:
        k = jnp.concatenate(
            [far_w[:, at : at + HV], wqk[:WB, lanes + at : lanes + at + HV]], axis=0
        )
        v = jnp.concatenate(
            [
                far_w[:, lanes + at : lanes + at + HV],
                rest[:WB, at : at + HV],
            ],
            axis=0,
        )
    start = REACH + b * WB
    back = (
        lax.broadcasted_iota(jnp.int32, (WB, 2 * WB), 0)
        + WB
        - lax.broadcasted_iota(jnp.int32, (WB, 2 * WB), 1)
    )
    same = docs_c[start : start + WB, :] == docs_r[:, start - WB : start + WB]
    return k, v, same & (back >= 0) & (back < WIN)


def window_probs(q, k, allowed):
    scores = jnp.where(allowed, mm_nt(q, k) * SCALE, MASKED)
    exponent = jnp.exp(scores - jnp.max(scores, axis=1, keepdims=True))
    return exponent / jnp.sum(exponent, axis=1, keepdims=True)


def backward_body(
    heads, tokens, wqk, rest, far_v, far_w, docs_c, docs_r, out, den, dout,
    *rest_refs,
):
    dwqk, drest, dfar_v, dfar_w, acc_v, acc_k, acc_wk, acc_wv = rest_refs[-8:]
    lanes = heads * HV
    lane_zero = (lax.broadcasted_iota(jnp.int32, (QB, HV), 1) == 0).astype(BF)
    dfar_v[:, lanes:] = jnp.zeros((REACH, dfar_v.shape[1] - lanes), BF)
    drest[:, 2 * lanes :] = jnp.zeros((tokens, drest.shape[1] - 2 * lanes), BF)
    for i in range(heads):
        at = i * HV
        qs, ks = 2 * lanes + i * FEAT, 2 * lanes + (heads + i) * FEAT
        fs = lanes + (heads + i) * FEAT
        acc_v[...] = jnp.zeros_like(acc_v)
        acc_k[...] = jnp.zeros_like(acc_k)
        acc_wk[...] = jnp.zeros_like(acc_wk)
        acc_wv[...] = jnp.zeros_like(acc_wv)
        for b in range(tokens // QB):
            rows = slice(b * QB, (b + 1) * QB)
            q = rest[rows, qs : qs + FEAT]
            docs_q = docs_r[:, REACH + b * QB : REACH + (b + 1) * QB]
            dlin = dout[rows, at : at + HV].astype(F32)
            inverse = 1.0 / den[rows, i : i + 1]
            mean = jnp.sum(dlin * out[rows, at : at + HV].astype(F32), axis=1, keepdims=True)
            dnumer = (dlin * inverse).astype(BF)
            ddenom = (-mean * inverse).astype(BF)
            extended = jnp.concatenate([dnumer, ddenom * lane_zero], axis=1)
            dq = jnp.zeros((QB, FEAT), F32)
            for kb in range(b - REACH // QB, b + 1):
                place = slice(REACH + kb * QB, REACH + (kb + 1) * QB)
                if kb >= 0:
                    keys = slice(kb * QB, (kb + 1) * QB)
                    k = rest[keys, ks : ks + FEAT]
                    v = rest[keys, lanes + at : lanes + at + HV]
                else:
                    k = far_v[place, fs : fs + FEAT]
                    v = far_v[place, at : at + HV]
                inner = mm_nt(k, q) * 0.25
                weight = mm_nt(jnp.concatenate([v, lane_zero], axis=1), extended)
                allowed = docs_c[place, :] == docs_q
                if kb == b:
                    allowed = allowed & (
                        lax.broadcasted_iota(jnp.int32, (QB, QB), 0)
                        <= lax.broadcasted_iota(jnp.int32, (QB, QB), 1)
                    )
                kernel = jnp.where(allowed, 1.0 + inner + 0.5 * inner * inner, 0.0).astype(BF)
                slope = jnp.where(allowed, weight * (0.25 + 0.25 * inner), 0.0).astype(BF)
                acc_v[place, :] += mm(kernel, dnumer)
                acc_k[place, :] += mm(slope, q)
                dq = dq + mm_tn(slope, k)
            drest[rows, qs : qs + FEAT] = dq.astype(BF)
        dfar_v[:, at : at + HV] = acc_v[:REACH, :].astype(BF)
        dfar_v[:, fs : fs + FEAT] = acc_k[:REACH, :].astype(BF)
        drest[:, lanes + at : lanes + at + HV] = acc_v[REACH:, :].astype(BF)
        drest[:, ks : ks + FEAT] = acc_k[REACH:, :].astype(BF)
        for b in range(tokens // WB):
            rows = slice(b * WB, (b + 1) * WB)
            q = wqk[rows, at : at + HV]
            k, v, allowed = window_block(b, at, lanes, wqk, rest, far_w, docs_c, docs_r)
            probs = window_probs(q, k, allowed)
            upstream = dout[rows, lanes + at : lanes + at + HV]
            dprobs = mm_nt(upstream, v)
            dscores = probs * (dprobs - jnp.sum(probs * dprobs, axis=1, keepdims=True))
            dscores = dscores.astype(BF)
            dwqk[rows, at : at + HV] = (mm(dscores, k) * SCALE).astype(BF)
            span = slice(b * WB, (b + 2) * WB)
            acc_wk[span, :] += mm_tn(dscores, q)
            acc_wv[span, :] += mm_tn(probs.astype(BF), upstream)
        dfar_w[:, at : at + HV] = (acc_wk[:WB, :] * SCALE).astype(BF)
        dfar_w[:, lanes + at : lanes + at + HV] = acc_wv[:WB, :].astype(BF)
        dwqk[:, lanes + at : lanes + at + HV] = (acc_wk[WB:, :] * SCALE).astype(BF)
        drest[:, at : at + HV] = acc_wv[WB:, :].astype(BF)


VMEM = pltpu.CompilerParams(vmem_limit_bytes=28 * 2**20)


def attention_forward(heads, wqk, rest, far_v, far_w, docs_c, docs_r, *earlier):
    tokens = wqk.shape[0]
    ins = (wqk, rest, far_v, far_w, docs_c, docs_r)
    outs = (
        jax.ShapeDtypeStruct((tokens, 2 * heads * HV), BF),
        jax.ShapeDtypeStruct((tokens, heads), F32),
    )
    return pl.pallas_call(
        functools.partial(forward_body, heads, tokens),
        in_specs=[pl.BlockSpec(memory_space=pltpu.VMEM)] * len(ins) + anywhere(len(earlier)),
        out_shape=outs,
        compiler_params=VMEM,
        cost_estimate=cost(6e9),
        name="attention_forward",
    )(*ins, *earlier)


def attention_backward(heads, wqk, rest, far_v, far_w, docs_c, docs_r, out, den, dout, *earlier):
    tokens = wqk.shape[0]
    ins = (wqk, rest, far_v, far_w, docs_c, docs_r, out, den, dout)
    return pl.pallas_call(
        functools.partial(backward_body, heads, tokens),
        in_specs=[pl.BlockSpec(memory_space=pltpu.VMEM)] * len(ins) + anywhere(len(earlier)),
        out_shape=tuple(jax.ShapeDtypeStruct(a.shape, BF) for a in (wqk, rest, far_v, far_w)),
        scratch_shapes=[
            pltpu.VMEM((REACH + tokens, HV), F32),
            pltpu.VMEM((REACH + tokens, FEAT), F32),
            pltpu.VMEM((WB + tokens, HV), F32),
            pltpu.VMEM((WB + tokens, HV), F32),
        ],
        compiler_params=VMEM,
        cost_estimate=cost(17e9),
        name="attention_backward",
    )(*ins, *earlier)


def feature_tables():
    pick_a = np.zeros((F1, F1 * F1), np.float32)
    pick_b = np.zeros((F1, F1 * F1), np.float32)
    scale = np.ones((F1 * F1,), np.float32)
    for r in range(F1):
        for j in range(F1):
            f = r * F1 + j
            pick_a[r, f] = 1.0
            if r < FEAT:
                scale[f] = HALF_ROOT
                if j < FEAT:
                    pick_b[j, f] = 1.0
            else:
                pick_b[FEAT if j == 0 else j - 1, f] = 1.0
    return pick_a, pick_b, scale


def row_states(heads, keys, values, docs):
    keys, values = keys[:, -REACH:], values[:, -REACH:]
    keys = jnp.swapaxes(keys.reshape(2, REACH, heads, FEAT), 1, 2).reshape(-1, REACH, FEAT)
    values = jnp.swapaxes(values.reshape(2, REACH, heads, HV), 1, 2).reshape(-1, REACH, HV)
    ones = jnp.ones(keys.shape[:2] + (1,), BF)
    extended = jnp.concatenate([keys * BF(0.5), ones], axis=2)
    pick_a, pick_b, scale = feature_tables()
    left = jnp.einsum("bsf,fg->bsg", extended, jnp.asarray(pick_a, BF), preferred_element_type=F32)
    right = jnp.einsum("bsf,fg->bsg", extended, jnp.asarray(pick_b, BF), preferred_element_type=F32)
    in_last = (docs[-REACH:] == docs[-1]).astype(F32)
    features = left * right * scale * in_last[None, :, None]
    return jnp.einsum("bsg,bsv->bgv", features.astype(BF), values, preferred_element_type=F32)


def owned_states(heads, states, owner):
    ways = lax.axis_size("t")
    mine_t, side = lax.axis_index("t"), lax.axis_index("s")
    states = lax.all_gather(states.astype(BF), ("c", "s"), axis=0, tiled=False)
    states = lax.dynamic_index_in_dim(states, 2 + lax.axis_index("c"), 0, False)
    states = lax.all_gather(states, "t", axis=0, tiled=False).reshape(GROUPS, F1, HV)
    slots = GROUPS // ways
    groups = jnp.arange(GROUPS, dtype=jnp.int32)
    mine = owner == 2 * mine_t + side
    ordinal = jnp.sum((mine[None, :] & (groups[None, :] < groups[:, None])).astype(jnp.int32), axis=1)
    wanted = jnp.arange(slots, dtype=jnp.int32)
    picked = (mine[None, :] & (ordinal[None, :] == wanted[:, None])).astype(BF)
    return jnp.einsum("kg,gfv->kfv", picked, states, preferred_element_type=F32)[None]


def momentum_update(weights, moment, average, gradient, factor, token_total):
    step_rate = factor / math.sqrt(token_total)
    moment_new = MOMENTUM * moment + gradient
    weights_new = weights - step_rate * (gradient + MOMENTUM * moment_new)
    average_new = AVERAGE_OLD * average + AVERAGE_NEW * weights_new
    return (gradient, weights_new, moment_new, average_new, weights_new.astype(BF))


def norm_back(values, factor, gains, upstream):
    gain_grad = jnp.sum(upstream * values, axis=0)
    inner = total_t(jnp.sum(upstream * gains * values, axis=1))
    scale = factor * factor * inner[:, None] / D
    return gains * upstream - values * scale, gain_grad


def local(
    layer_in, out_grad, doc_ids, group_owner,
    norm_gains, norm_gains_moment, norm_gains_average,
    feature_proj, feature_proj_moment, feature_proj_average,
    head_proj, head_proj_moment, head_proj_average,
    mixer_out, mixer_out_moment, mixer_out_average,
    gate_up, gate_up_moment, gate_up_average,
    down_proj, down_proj_moment, down_proj_average,
):
    data_ways = lax.axis_size("y") * 2
    core, side = lax.axis_index("c"), lax.axis_index("s")
    width = layer_in.shape[1]
    tokens = layer_in.shape[0] // 2
    heads = head_proj.shape[2] // HV
    rows = head_proj.shape[0]
    lanes = heads * HV
    token_total = layer_in.shape[0] * data_ways

    x_low = enter(layer_in)
    x = x_low.astype(F32)
    other_gains = lax.ppermute(norm_gains, "s", [(0, 1), (1, 0)])
    gains = jnp.where(
        side == 0,
        jnp.concatenate([norm_gains, other_gains], axis=1),
        jnp.concatenate([other_gains, norm_gains], axis=1),
    )
    docs = lax.ppermute(doc_ids, ("c", "s"), SWAP)
    docs = jnp.concatenate([jnp.full((1, REACH), -1, jnp.int32), docs], axis=1)
    docs_r = lax.dynamic_slice_in_dim(docs, core * tokens, REACH + tokens, 1)
    docs_c = jnp.reshape(docs_r, (REACH + tokens, 1))

    scaled_mine = (x * gains[0]).astype(BF)
    wqk_shard = head_proj[:, :2].reshape(rows, -1)
    extra = -(2 * heads * FEAT) % HV
    rest_shard = jnp.concatenate(
        [head_proj[:, 2:].reshape(rows, -1), feature_proj.reshape(rows, -1), jnp.zeros((rows, extra), F32)], axis=1
    )
    parts = send_t(scaled_mine)
    wqk_full = rows_of(gather_weight(rounded(wqk_shard, x_low)))
    rest_full = rows_of(gather_weight(rounded(rest_shard, x_low)))
    begun = parts[1:3]
    mixer_shard = rounded(jnp.transpose(mixer_out, (2, 0, 1)).reshape(rows, -1), *begun)
    down_shard = rounded(down_proj, *begun)
    both_shard = packed_rounded(gate_up, *begun)
    mixer_full = rows_of(gather_weight(mixer_shard))
    down_full = gather_weight(down_shard)
    both_full = rows_of(gather_weight(both_shard))
    factor_one = lax.rsqrt(total_t(jnp.sum(x * x, axis=1)) / D + EPSILON)[:, None]
    scaled_one = join_t(parts, mixer_shard, down_shard, both_shard)
    dy_mine = hold(enter(out_grad, *begun), scaled_one)
    dy = lax.all_gather(dy_mine, "t", axis=1, tiled=True)
    wqk, rest = [], []
    for s in range(2):
        one, two = project(scaled_one, [(wqk_full, s), (rest_full, s)], factor_one)
        wqk.append(one)
        rest.append(two)

    ahead, behind = [(0, 1)], [(1, 0)]
    far_v = [lax.ppermute(p[-REACH:, lanes:], "c", ahead) for p in rest]
    far_w = [
        lax.ppermute(jnp.concatenate([a[-WB:, lanes:], b[-WB:, :lanes]], axis=1), "c", ahead)
        for a, b in zip(wqk, rest)
    ]
    attended, denom = [], []
    for s in range(2):
        one, two = attention_forward(heads, wqk[s], rest[s], far_v[s], far_w[s], docs_c, docs_r)
        attended.append(one)
        denom.append(two)

    parts, second = spread_t(attended, both_s(mixer_full))
    dhidden = [back_hidden(dy, down_full, s) for s in range(2)]
    mixed = add_up([hold(parts[0], *dhidden)] + parts[1:])
    middle = x + mixed
    factor_two = lax.rsqrt(total_t(jnp.sum(middle * middle, axis=1)) / D + EPSILON)[:, None]
    scaled_mine = (middle * gains[1]).astype(BF)
    parts = send_t(scaled_mine)
    last = hold(jnp.stack([p[-REACH:, lanes:] for p in rest]), *second[:2])
    states = row_states(heads, last[:, :, lanes + heads * FEAT : lanes + 2 * heads * FEAT], last[:, :, :lanes], docs_r[0])
    scaled_two = join_t(parts, states)
    row_state = owned_states(heads, hold(states, scaled_two), group_owner)

    hidden, dboth = [], []
    for s in range(2):
        one, two = feed_forward(scaled_two, factor_two, dhidden[s], both_full, s)
        hidden.append(one)
        dboth.append(two)
    parts, second = spread_t(dboth, both_s(both_full))
    for_down = down_grads(dy, hidden, *second[:2])
    pieces = pieces_t(hidden, both_s(down_full), *second[:2]) if line() else []
    upstream_two = add_up([hold(parts[0], for_down, *pieces)] + parts[1:])
    back_two, gain_two = norm_back(middle, factor_two, gains[1], upstream_two)
    dmixed_mine = (dy_mine.astype(F32) + back_two).astype(BF)
    parts = send_t(dmixed_mine)
    for_both = grads(scaled_two, dboth, *parts[1:3])
    if line():
        first = hold(pieces[0], *parts[3:5])
        branch_parts, second = along_line(first, *pieces[1:])
        second = [first] + second
    else:
        branch_parts, second = spread_t(hidden, both_s(down_full))
    dmixed = join_t(parts, for_both)
    down_sum, both_sum = scatter_grad(for_down), scatter_grad(for_both)

    branch = add_up(branch_parts)
    out_y = layer_in + leave((mixed + branch).astype(BF)).astype(F32)
    dattended = project(dmixed, both_s(mixer_full), jnp.ones((tokens, 1), F32), *second[1:3])
    mixer_sum = scatter_grad(grads(dmixed, attended, *dattended))
    dwqk, drest = [], []
    for s in range(2):
        one, two, three, four = attention_backward(
            heads, wqk[s], rest[s], far_v[s], far_w[s], docs_c, docs_r, attended[s], denom[s], dattended[s], *([row_state] if s else second[3:5])
        )
        far_three = lax.ppermute(three, "c", behind).astype(F32)
        far_four = lax.ppermute(four, "c", behind).astype(F32)
        one = one.astype(F32) + jnp.pad(far_four[:, :lanes], ((tokens - WB, 0), (lanes, 0)))
        two = (
            two.astype(F32)
            + jnp.pad(far_three, ((tokens - REACH, 0), (lanes, 0)))
            + jnp.pad(far_four[:, lanes:], ((tokens - WB, 0), (0, rest[s].shape[1] - lanes)))
        )
        dwqk.append((one * factor_one).astype(BF))
        drest.append((two * factor_one).astype(BF))
    for_rest = grads(scaled_one, drest, branch)
    for_wqk = grads(scaled_one, dwqk, for_rest)
    rest_sum, wqk_sum = scatter_grad(for_rest), scatter_grad(for_wqk)
    parts, second = spread_t(dwqk + drest, both_s(wqk_full) + both_s(rest_full), for_wqk, both_sum)
    upstream_one = add_up(parts)
    back_one, gain_one = norm_back(x, factor_one, gains[0], upstream_one)
    back = (back_one + back_two).astype(BF)
    grad_x = out_grad + leave(back).astype(F32)
    both_sum, down_sum = [hold(a, *second[:1]) for a in (both_sum, down_sum)]
    wqk_sum, rest_sum, mixer_sum = [hold(a, back) for a in (wqk_sum, rest_sum, mixer_sum)]
    wqk_sum, rest_sum, mixer_sum, both_sum = [a.astype(F32) for a in (wqk_sum, rest_sum, mixer_sum, both_sum)]
    down_sum = down_sum[0].astype(F32)
    head_sum = jnp.concatenate([wqk_sum, rest_sum[:, : 2 * lanes]], axis=1)
    feature_sum = rest_sum[:, 2 * lanes : 2 * lanes + 2 * heads * FEAT]

    both = jnp.stack([gain_one, gain_two], axis=0)
    both = both + peer(both, "c", 1)
    step = 1
    while step < data_ways // 2:
        both = both + peer(both, "y", step)
        step *= 2
    low, high = both[:, :width], both[:, width:]
    gains_sum = jnp.where(side == 0, low, high) + peer(jnp.where(side == 0, high, low), "s", 1)

    mixer_sum = jnp.transpose(mixer_sum.reshape(rows, 2, lanes), (1, 2, 0))
    triples = (
        (norm_gains, norm_gains_moment, norm_gains_average, gains_sum),
        (feature_proj, feature_proj_moment, feature_proj_average, feature_sum.reshape(feature_proj.shape)),
        (head_proj, head_proj_moment, head_proj_average, head_sum.reshape(head_proj.shape)),
        (mixer_out, mixer_out_moment, mixer_out_average, mixer_sum),
        (gate_up, gate_up_moment, gate_up_average, jnp.stack(unpack(both_sum), axis=1)),
        (down_proj, down_proj_moment, down_proj_average, down_sum),
    )
    results = [out_y, grad_x, row_state]
    for index, triple in enumerate(triples):
        results.extend(momentum_update(*triple, RATE_FACTORS[index], token_total))
    return tuple(results)


def solution(mesh):
    data_ways, model_ways = mesh.shape["dp"], mesh.shape["mp"]
    grid = Mesh(mesh.devices.reshape(data_ways // 2, 2, model_ways // 2, 2), ("y", "c", "t", "s"))
    dp, mp = ("y", "c"), ("t", "s")
    gains = (P(None, mp),)
    rows_cols = (P(dp, None, mp),)
    mixer = (P(None, mp, dp),)
    down = (P(mp, dp),)
    tokens = (P(dp, mp),)
    return jax.shard_map(
        local,
        mesh=grid,
        in_specs=tokens * 2
        + (P(dp, None), P())
        + gains * 3
        + rows_cols * 6
        + mixer * 3
        + rows_cols * 3
        + down * 3,
        out_specs=tokens * 2
        + (P(dp, mp, None, None),)
        + gains * 5
        + rows_cols * 10
        + mixer * 5
        + rows_cols * 5
        + down * 5,
        check_vma=False,
    )
```
